256 devices in a mesh: clusters: 64 (over z, x, core), tiles: 4 (over y).
Axes of the slice: x: 4, y: 4, z: 8, core: 2. Of those that a mesh axis runs over, the one named last changes fastest.
Arguments:
- source_points: bfloat16 [512, 30, 1024], P('clusters', None, 'tiles'), may hold values from -1.5 to 1.5
- target_points: bfloat16 [512, 30, 1024], P('clusters'), may hold values from -1.5 to 1.5
- source_potential: float32 [512, 1024], P('clusters', 'tiles'), may hold values from -66 to 66
- target_potential: float32 [512, 1024], P('clusters'), may hold values from -66 to 66
- kept_targets: int32 [512, 12], replicated, may hold values from 0 to 511, as said below
- kept_counts: int32 [512], replicated, may hold values from 1 to 12, as said below
- target_home: int32 [512], replicated, may hold values from 0 to 511, as said below
Outputs:
- source_next: float32 [512, 1024], P('clusters', 'tiles')
- target_next: float32 [512, 1024], P('clusters')
The draws below stay inside these ranges and needn't reach their ends.
Inputs may be any that keep to these rules, and one draw needn't show every extreme that they name: `kept_counts`: every source cluster has one or more live slots; on every index of clusters one of its 8 source clusters has all 12. `kept_targets`: the 12 slots of a source cluster name distinct clusters. Call the slots of the 8 source clusters of one index of clusters one requester, and target_home[id] // 8 the owner of the cluster a slot names: the slots of one requester name at most 2 clusters of any one owner, live or not; in every draw one owner is named by 2 live slots of every requester. `target_home`: A permutation of the target cluster ids.
All inputs are finite; a program needn't handle non-finite values.
Results may differ from the reference program's by a relative error of at most 0.002.
Values may be sent and summed in bfloat16 or wider, within the bound.
A program may use at most 64 MiB of HBM per device.

```python
import jax
import jax.numpy as jnp
from jax import lax

DIM = 30
CL = 1024
KMAX = 12
SPD = 8
ITERS = 1
CAP = 2
TPD = 8
NS = 512
NT = 512
N_TILES = 4


def kept_tables(base_key):
    groups = NS // SPD
    slot_count = SPD * KMAX
    item_count = groups * CAP
    key_counts, key_full, key_favored, key_order, key_lane, key_home = jax.random.split(base_key, 6)
    counts = jax.random.randint(key_counts, (groups, SPD), 1, KMAX + 1)
    full_at = jax.random.randint(key_full, (groups, 1), 0, SPD)
    counts = jnp.where(jnp.arange(SPD)[None, :] == full_at, KMAX, counts)
    living = jnp.arange(KMAX)[None, None, :] < counts[:, :, None]
    living = living.reshape(groups, slot_count)
    slot_index = jnp.arange(slot_count)
    live_score = jnp.where(living, 0, slot_count) + slot_index[None, :]
    live_place = jnp.argsort(jnp.argsort(live_score, axis=-1), axis=-1)
    favored = jax.random.randint(key_favored, (), 0, groups)
    group_keys = jax.random.split(key_order, groups)
    shuffled = jax.vmap(lambda one_key: jax.random.permutation(one_key, item_count))(group_keys)
    priority = jnp.where(shuffled // CAP == favored, 0, item_count) + jnp.arange(item_count)[None, :]
    sequence = jnp.take_along_axis(shuffled, jnp.argsort(priority, axis=-1), axis=-1)
    chosen = jnp.take_along_axis(sequence, live_place, axis=-1)
    lanes = jax.random.randint(key_lane, (groups, item_count), 0, N_TILES)
    lane_of = jnp.take_along_axis(lanes, chosen, axis=-1)
    local_index = chosen % CAP * N_TILES + lane_of
    stored = chosen // CAP * TPD + local_index
    stored = stored.reshape(NS, KMAX)
    home_perm = jax.random.permutation(key_home, NT)
    logical = jnp.argsort(home_perm)[stored]
    return (logical.astype(jnp.int32), counts.reshape(NS).astype(jnp.int32), home_perm.astype(jnp.int32))


def draw_kept_targets(key, part):
    return kept_tables(key)[0]


def draw_kept_counts(key, part):
    return kept_tables(key)[1]


def draw_target_home(key, part):
    return kept_tables(key)[2]


def draw_source_potential(key, part):
    key = jax.random.fold_in(key, 12)
    key_base = jax.random.fold_in(key, 0)
    potential = jnp.clip(0.3 * jax.random.normal(key_base, (NS, CL), jnp.float32), -1.8, 1.8)
    return potential


def draw_target_potential(key, part):
    key = jax.random.fold_in(key, 11)
    key_base = jax.random.fold_in(key, 0)
    potential = jnp.clip(0.3 * jax.random.normal(key_base, (NT, CL), jnp.float32), -1.8, 1.8)
    return potential


def level_of(stream_key, shape, pieces, low, high):
    def one(axis_at, shards_of):
        steps = jax.random.uniform(jax.random.fold_in(jax.random.fold_in(stream_key, 6), axis_at), (shards_of,), jnp.float32, low / len(pieces), high / len(pieces))
        return jnp.repeat(jnp.exp(steps), shape[axis_at] // shards_of).reshape((-1,) + (1,) * (len(shape) - axis_at - 1))

    factor_of = one(*pieces[0])
    for cut in pieces[1:]:
        factor_of = factor_of * one(*cut)
    return factor_of


def centred(stream_key, shape, width, limit, pieces=(), kind=jnp.bfloat16):
    array = width * jax.random.normal(stream_key, shape, jnp.float32)
    if pieces:
        array = array * level_of(stream_key, shape, pieces, -0.22, 0.18)
    return jnp.clip(array, -limit, limit).astype(kind)


def setup_inputs(seed: int = 0) -> dict:
    splits = jax.random.split(jax.random.key(seed), 8)
    source_points = centred(splits[0], (NS, DIM, CL), 0.25, 1.5, ((0, 64), (2, 4)))
    target_points = centred(splits[1], (NT, DIM, CL), 0.25, 1.5, ((0, 64),))
    source_potential = draw_source_potential(jax.random.fold_in(splits[7], 71), 0)
    target_potential = draw_target_potential(jax.random.fold_in(splits[7], 71), 0)
    kept_targets = draw_kept_targets(jax.random.fold_in(splits[7], 71), 0)
    kept_counts = draw_kept_counts(jax.random.fold_in(splits[7], 71), 0)
    target_home = draw_target_home(jax.random.fold_in(splits[7], 71), 0)
    return {"source_points": source_points, "target_points": target_points, "source_potential": source_potential, "target_potential": target_potential, "kept_targets": kept_targets, "kept_counts": kept_counts, "target_home": target_home}


epsilon_reg = 0.25
sentinel = -1.0e30


def lse_pair(first, second):
    summit = jnp.maximum(first[0], second[0])
    return (summit, first[1] * jnp.exp(first[0] - summit) + second[1] * jnp.exp(second[0] - summit))


def one_sweep(source_points, target_points, source_norms, target_norms, stored, living, source_now, target_now):
    cluster_width = source_points.shape[2]

    def per_source(carry, source_index):
        points = source_points[source_index]
        point_norms = source_norms[source_index]
        potential = source_now[source_index]

        def per_slot(slot_index, state):
            target_index = stored[source_index, slot_index]

            def take_tile(inner):
                row_peak, row_mass, col_peak, col_mass = inner
                inner_prod = jnp.dot(points.T, target_points[target_index], preferred_element_type=jnp.float32)
                tile_cost = 0.5 * point_norms[:, None] + 0.5 * target_norms[target_index][None, :] - inner_prod
                row_scores = (target_now[target_index][None, :] - tile_cost) / epsilon_reg
                row_top = jnp.max(row_scores, axis=1)
                row_sum = jnp.sum(jnp.exp(row_scores - row_top[:, None]), axis=1)
                row_peak, row_mass = lse_pair((row_peak, row_mass), (row_top, row_sum))
                col_scores = (potential[:, None] - tile_cost) / epsilon_reg
                col_top = jnp.max(col_scores, axis=0)
                col_sum = jnp.sum(jnp.exp(col_scores - col_top[None, :]), axis=0)
                merged = lse_pair((col_peak[target_index], col_mass[target_index]), (col_top, col_sum))
                return (row_peak, row_mass, col_peak.at[target_index].set(merged[0]), col_mass.at[target_index].set(merged[1]))

            return lax.cond(living[source_index, slot_index], take_tile, lambda inner: inner, state)

        start = (jnp.full((cluster_width,), sentinel, jnp.float32), jnp.zeros((cluster_width,), jnp.float32), carry[0], carry[1])
        row_peak, row_mass, col_peak, col_mass = lax.fori_loop(0, KMAX, per_slot, start)
        return (col_peak, col_mass), -epsilon_reg * (row_peak + jnp.log(row_mass))

    begin = (jnp.full(target_now.shape, sentinel, jnp.float32), jnp.zeros(target_now.shape, jnp.float32))
    (col_peak, col_mass), source_next = lax.scan(per_source, begin, jnp.arange(NS, dtype=jnp.int32))
    reached = col_mass > 0
    target_next = jnp.where(reached, -epsilon_reg * (col_peak + jnp.log(jnp.where(reached, col_mass, 1.0))), target_now)
    return source_next, target_next


def reference(source_points, target_points, source_potential, target_potential, kept_targets, kept_counts, target_home):
    source_norms = jnp.sum(jnp.square(source_points.astype(jnp.float32)), axis=1)
    target_norms = jnp.sum(jnp.square(target_points.astype(jnp.float32)), axis=1)
    stored = target_home[kept_targets]
    living = jnp.arange(KMAX, dtype=jnp.int32)[None, :] < kept_counts[:, None]
    source_now = source_potential
    target_now = target_potential
    for sweep_step in range(ITERS):
        source_now, target_now = one_sweep(source_points, target_points, source_norms, target_norms, stored, living, source_now, target_now)
    return source_now, target_now
```

```python
import functools

import jax
import jax.numpy as jnp
from jax import lax
from jax.experimental import pallas as pl
from jax.experimental.pallas import tpu as pltpu
from jax.sharding import PartitionSpec as P

MESH = pl.DeviceIdType.MESH
ZS, XS, YS = 8, 4, 4
PER = 8
SHARP = 4.0
EXP2_SCALE = 5.770780163555854
LOW = -1e30
SOURCES, TARGETS = XS * 2 * PER, ZS * 2 * PER
LIST = 256
UNROLL = 8
F32, BF16, I32 = jnp.float32, jnp.bfloat16, jnp.int32


def place():
    c, y = lax.axis_index("clusters"), lax.axis_index("tiles")
    return c // 8, (c // 2) % 4, c % 2, y


def device(z, x, k, y):
    return (z * 8 + x * 2 + k, y)


def iota(shape, dim):
    return lax.broadcasted_iota(I32, shape, dim)


def widen(points, potential, work, out):
    values = points[...].astype(F32)
    half_norm = 0.5 * jnp.sum(values * values, axis=1)
    term = potential[...] - half_norm
    high = term.astype(BF16).astype(F32)
    low = (term - high).astype(BF16).astype(F32)
    work[:, 0:30, :] = values
    work[:, 30:31, :] = high[:, None, :]
    work[:, 31:32, :] = low[:, None, :]
    out(work[...].astype(BF16))
    return high + low + half_norm


def edge_list(z, x, kept, counts, home, edges_ref, has_row_ref, has_col_ref):
    lane = iota((SOURCES, 512), 1)
    row = iota((SOURCES, 512), 0)
    count = jnp.sum(jnp.where(lane == row + z * SOURCES, counts[...].astype(F32), 0.0), axis=1, keepdims=True)
    names = kept[...]
    homes = home[...].astype(F32)
    own_row = iota((SOURCES, 1), 0)
    codes, marks, before, total = [], [], [], jnp.zeros((SOURCES, 1), F32)
    for k in range(12):
        at = jnp.sum(jnp.where(names[:, k:k + 1] == lane, homes, 0.0), axis=1, keepdims=True).astype(I32)
        mark = jnp.where((count > float(k)) & (((at >> 4) & 3) == x), 1.0, 0.0)
        codes.append((own_row * TARGETS + ((at >> 6) << 4) + (at & 15) + 1).astype(F32))
        marks.append(mark)
        before.append(total)
        total = total + mark
    square_row, square_lane = iota((SOURCES, SOURCES), 0), iota((SOURCES, SOURCES), 1)
    across = jnp.sum(jnp.where(square_row == square_lane, total, 0.0), axis=0, keepdims=True)
    ahead = jnp.sum(jnp.where(square_lane < square_row, across, 0.0), axis=1, keepdims=True)
    slot = iota((SOURCES, LIST), 1).astype(F32)
    filled = jnp.zeros((SOURCES, LIST), F32)
    for code, mark, prior in zip(codes, marks, before):
        filled = filled + jnp.where((slot == ahead + prior) & (mark > 0.0), code, 0.0)
    listed = jnp.sum(filled, axis=0, keepdims=True)
    number = jnp.sum(total, axis=0, keepdims=True)
    chosen = jnp.where(listed > 0.0, listed - 1.0, float(SOURCES * TARGETS)).astype(I32)
    edges_ref[...] = jnp.where(iota((8, LIST), 0) == 0, chosen, number.astype(I32))
    has_row_ref[...] = jnp.broadcast_to(jnp.where(total > 0.0, 1.0, 0.0), has_row_ref.shape)
    named = (iota((TARGETS, LIST), 0) == (chosen & (TARGETS - 1))) & (listed > 0.0)
    has_col_ref[...] = jnp.broadcast_to(
        jnp.max(jnp.where(named, 1.0, 0.0), axis=1, keepdims=True), has_col_ref.shape)


def collect_kernel(sp_hbm, tp_hbm, f_hbm, g_hbm, kept_hbm, counts_hbm, home_hbm,
                   src, turned, edges_ref, has_row_ref, has_col_ref, src_base, tgt_base, kept_pot,
                   sp, tp, f, g, kept, counts, home, work, spare, tgt,
                   load_sem, send_sem, recv_sem):
    z, x, k, y = place()
    step = lambda at, by, n: lax.rem(at + (by + n), n)

    loads = [
        pltpu.make_async_copy(a, b, load_sem.at[i])
        for i, (a, b) in enumerate([
            (sp_hbm, sp),
            (f_hbm, f),
            (tp_hbm.at[:, :, pl.ds(pl.multiple_of(y * 256, 256), 256)], tp),
            (g_hbm.at[:, pl.ds(pl.multiple_of(y * 256, 256), 256)], g),
            (kept_hbm.at[pl.ds(pl.multiple_of(z * SOURCES, SOURCES), SOURCES), :], kept),
            (counts_hbm, counts),
            (home_hbm, home),
        ])
    ]
    for load in loads:
        load.start()

    mate = device(z, x, 1 - k, y)
    xn = {d: device(z, step(x, d, XS), k, y) for d in (1, -1)}
    yn = {d: device(z, x, k, step(y, d, YS)) for d in (1, -1)}
    zn = {d: device(step(z, d, ZS), x, k, y) for d in (1, -1)}

    barrier = pltpu.get_barrier_semaphore()
    for other in (mate, xn[1], xn[-1], yn[1], yn[-1], zn[1], zn[-1]):
        pl.semaphore_signal(barrier, inc=1, device_id=other, device_id_type=MESH)

    numbers = {}
    pending = []

    def descriptor(key, ref, to):
        m = numbers.setdefault(key, len(numbers))
        return pltpu.make_async_remote_copy(
            src_ref=ref, dst_ref=ref, send_sem=send_sem.at[m], recv_sem=recv_sem.at[m],
            device_id=to, device_id_type=MESH)

    def send(key, ref, to):
        copy = descriptor(key, ref, to)
        copy.start()
        pending.append(copy)

    def arrive(key, ref):
        descriptor(key, ref, mate).wait_recv()

    def src_block(dx, dy, q, lo=0, n=PER):
        return src.at[step(y, dy, YS), pl.ds(step(x, dx, XS) * 16 + q * 8 + lo, n)]

    loads[0].wait()
    loads[1].wait()

    def put_source(block):
        halves = block[:, :, 0:128], block[:, :, 128:256]
        src[y, pl.ds(x * 16 + k * 8, PER)] = jnp.where(k == 0, halves[0], halves[1])
        spare[...] = jnp.where(k == 0, halves[1], halves[0])

    src_base[...] = widen(sp, f, work, put_source)
    pl.semaphore_wait(barrier, 7)
    cross = pltpu.make_async_remote_copy(
        src_ref=spare, dst_ref=src.at[y, pl.ds(x * 16 + k * 8, PER)],
        send_sem=send_sem.at[numbers.setdefault("cross", len(numbers))],
        recv_sem=recv_sem.at[numbers["cross"]], device_id=mate, device_id_type=MESH)
    cross.start()
    pending.append(cross)

    loads[2].wait()
    loads[3].wait()

    def put_target(block):
        tgt[z, k] = block

    tgt_base[...] = widen(tp, g, work, put_target)
    kept_pot[...] = g[...]

    def tgt_chunk(dz, c, core):
        return tgt.at[step(z, dz, ZS), core, pl.ds(c * 4, 4)]

    wide_id = iota((32, 256), 0)
    tail_id = iota((16, 256), 0)

    def turn(dz, c, core):
        zz = step(z, dz, ZS)

        def one(i, _):
            block = tgt[zz, core, c * 4 + i].astype(F32)
            top = jnp.where(wide_id < 30, block, 1.0)
            low = jnp.where(tail_id >= 14, block[16:32], 0.0)
            turned[zz * 16 + core * 8 + c * 4 + i] = jnp.concatenate([top, low], axis=0).T.astype(BF16)
            return 0

        lax.fori_loop(0, 4, one, 0, unroll=4)

    def pass_target(dz, c, forward):
        for d in forward:
            send(("z", d, dz, c), tgt_chunk(dz, c, k), zn[d])
        send(("m", dz, c), tgt_chunk(dz, c, k), mate)

    def take_target(d, dz, c, forward):
        arrive(("z", d, dz + d, c), tgt_chunk(dz, c, k))
        for e in forward:
            send(("z", e, dz, c), tgt_chunk(dz, c, k), zn[e])
        send(("m", dz, c), tgt_chunk(dz, c, k), mate)

    def take_mate(dz, c):
        arrive(("m", dz, c), tgt_chunk(dz, c, 1 - k))
        turn(dz, c, 1 - k)

    def off(q, first, second):
        return (first, second) if q == 0 else (second, first)

    near = {0: (xn, yn), 1: (yn, xn)}

    def first_out(q):
        for d in (1, -1):
            send(("a", q, d), src_block(0, 0, q), near[q][0][d])

    def first_in(q, d):
        dx, dy = off(q, -d, 0)
        arrive(("a", q, d), src_block(dx, dy, q))
        lo = 0 if d == 1 else 4
        send(("af", q, d), src_block(dx, dy, q, lo, 4), near[q][0][d])

    def first_far(q):
        dx, dy = off(q, 2, 0)
        for d in (1, -1):
            arrive(("af", q, d), src_block(dx, dy, q, 0 if d == 1 else 4, 4))

    def second_out(q, e):
        dx, dy = off(q, e, 0)
        for d in (1, -1):
            send(("b", q, e, d), src_block(dx, dy, q), near[q][1][d])

    def second_in(q, e):
        for d in (1, -1):
            dx, dy = off(q, e, -d)
            arrive(("b", q, e, d), src_block(dx, dy, q))
            send(("bf", q, e, d), src_block(dx, dy, q, 0 if d == 1 else 4, 4), near[q][1][d])

    def second_far(q, e):
        dx, dy = off(q, e, 2)
        for d in (1, -1):
            arrive(("bf", q, e, d), src_block(dx, dy, q, 0 if d == 1 else 4, 4))

    for c, d in ((0, 1), (1, -1)):
        send(("z", d, 0, c), tgt_chunk(0, c, k), zn[d])
    for c, d in ((1, 1), (0, -1)):
        send(("z", d, 0, c), tgt_chunk(0, c, k), zn[d])
    pltpu.make_async_remote_copy(
        src_ref=spare, dst_ref=src.at[y, pl.ds(x * 16 + (1 - k) * 8, PER)],
        send_sem=send_sem.at[numbers["cross"]], recv_sem=recv_sem.at[numbers["cross"]],
        device_id=mate, device_id_type=MESH).wait_recv()
    for q in (0, 1):
        first_out(q)
    for q in (0, 1):
        second_out(q, 0)
    for c in (0, 1):
        send(("m", 0, c), tgt_chunk(0, c, k), mate)
    for load in loads[4:]:
        load.wait()
    edge_list(z, x, kept, counts, home, edges_ref, has_row_ref, has_col_ref)
    idle = iota((32, 128), 0)
    for at in range(YS):
        src[at, SOURCES] = jnp.where(idle == 30, LOW, 0.0).astype(BF16)

    take_target(1, -1, 0, (1,))
    take_target(-1, 1, 1, (-1,))
    for q in (0, 1):
        for d in (1, -1):
            first_in(q, d)
        for e in (-1, 1):
            second_out(q, e)
    for c in (0, 1):
        turn(0, c, k)
    take_target(1, -1, 1, (1,))
    take_target(-1, 1, 0, (-1,))
    for q in (0, 1):
        second_in(q, 0)
    turn(-1, 0, k)
    turn(1, 1, k)
    take_mate(0, 0)
    take_mate(0, 1)
    take_target(1, -2, 0, (1,))
    take_target(-1, 2, 1, (-1,))
    for q in (0, 1):
        first_far(q)
        second_out(q, 2)
    turn(-1, 1, k)
    turn(1, 0, k)
    take_mate(-1, 0)
    take_mate(1, 1)
    take_target(1, -2, 1, (1,))
    take_target(-1, 2, 0, (-1,))
    for q in (0, 1):
        second_in(q, -1)
    turn(-2, 0, k)
    turn(2, 1, k)
    take_mate(-1, 1)
    take_mate(1, 0)
    take_target(1, -3, 0, (1,))
    take_target(-1, 3, 1, (-1,))
    for q in (0, 1):
        second_in(q, 1)
    turn(-2, 1, k)
    turn(2, 0, k)
    take_mate(-2, 0)
    take_mate(2, 1)
    take_target(1, -3, 1, ())
    take_target(-1, 3, 0, ())
    for q in (0, 1):
        second_in(q, 2)
    turn(-3, 0, k)
    turn(3, 1, k)
    take_mate(-2, 1)
    take_mate(2, 0)
    take_target(1, -4, 0, ())
    take_target(-1, 4, 1, ())
    turn(-3, 1, k)
    turn(3, 0, k)
    take_mate(-3, 0)
    take_mate(3, 1)
    turn(-4, 0, k)
    turn(4, 1, k)
    take_mate(-3, 1)
    take_mate(3, 0)
    take_mate(-4, 0)
    take_mate(4, 1)
    for q in (0, 1):
        for e in (0, -1, 1, 2):
            second_far(q, e)
    for copy in pending:
        copy.wait_send()


MESSAGES = 96


def collect(sp, tp, f, g, kept, counts, home):
    anyspace = pl.BlockSpec(memory_space=pl.ANY)
    vmem = pl.BlockSpec(memory_space=pltpu.VMEM)
    shape = jax.ShapeDtypeStruct
    return pl.pallas_call(
        collect_kernel,
        out_shape=(
            shape((YS, SOURCES + 1, 32, 128), BF16),
            shape((TARGETS, 256, 48), BF16),
            shape((8, LIST), I32),
            shape((SOURCES, 128), F32),
            shape((TARGETS, 128), F32),
            shape((PER, 256), F32),
            shape((PER, 256), F32),
            shape((PER, 256), F32),
        ),
        in_specs=[anyspace] * 7,
        out_specs=(vmem,) * 8,
        scratch_shapes=[
            pltpu.VMEM((PER, 30, 256), BF16),
            pltpu.VMEM((PER, 30, 256), BF16),
            pltpu.VMEM((PER, 256), F32),
            pltpu.VMEM((PER, 256), F32),
            pltpu.VMEM((SOURCES, 12), I32),
            pltpu.VMEM((1, 512), I32),
            pltpu.VMEM((1, 512), I32),
            pltpu.VMEM((PER, 32, 256), F32),
            pltpu.VMEM((PER, 32, 128), BF16),
            pltpu.VMEM((ZS, 2, PER, 32, 256), BF16),
            pltpu.SemaphoreType.DMA((7,)),
            pltpu.SemaphoreType.DMA((MESSAGES,)),
            pltpu.SemaphoreType.DMA((MESSAGES,)),
        ],
        compiler_params=pltpu.CompilerParams(
            collective_id=0, has_side_effects=True, vmem_limit_bytes=32 * 2**20),
        name="collect",
    )(sp, tp, f, g, kept, counts, home)


def tiles_kernel(edge_vmem, src, turned, has_row_ref, has_col_ref, row_ref, col_ref,
                 edge_ref, row_acc, col_acc, edge_sem):
    load = pltpu.make_async_copy(edge_vmem, edge_ref, edge_sem)
    load.start()
    width = turned.shape[1]
    tail = jnp.where(iota((16, YS * 128), 0) >= 14, 1.0, 0.0).astype(BF16)
    row_acc[...] = jnp.zeros(row_acc.shape, F32)
    col_acc[...] = jnp.zeros(col_acc.shape, F32)
    load.wait()
    count = edge_ref[1, 0]

    def scores(s, p):
        cells = jnp.concatenate([src[at, s] for at in range(YS)], axis=1)
        right = jnp.concatenate([cells, tail], axis=0)
        return jnp.dot(turned[p], right, preferred_element_type=F32)

    def step(it, _):
        got = []
        for u in range(UNROLL):
            code = edge_ref[0, it * UNROLL + u]
            s, p = code // TARGETS, code % TARGETS
            e = jnp.exp2(scores(s, p) * EXP2_SCALE)
            rows = e.reshape(width // 8, 8, YS * 128).sum(axis=0)
            q = (e[:, 0:128] + e[:, 128:256]) + (e[:, 256:384] + e[:, 384:512])
            got.append((s, p, rows, q.T.reshape(16, 8, width).sum(axis=0)))
        for s, p, rows, cols in got:
            row_acc[s] += rows
            col_acc[p] += cols
        return 0

    lax.fori_loop(0, (count + UNROLL - 1) // UNROLL, step, 0)

    row_sum = jnp.sum(row_acc[0:SOURCES], axis=1)
    col_sum = jnp.sum(col_acc[...], axis=1)
    has_row = has_row_ref[:, 0:1] > 0.0
    has_col = has_col_ref[:, 0:1] > 0.0

    def outside(has, total):
        good = (total >= 2.0**-90) & (total <= 2.0**120)
        return jnp.max(jnp.where(has & jnp.logical_not(good), 1.0, 0.0))

    row_ref[...] = jnp.where(has_row, jnp.log(jnp.where(has_row, row_sum, 1.0)), LOW)
    col_ref[...] = jnp.where(has_col, jnp.log(jnp.where(has_col, col_sum, 1.0)), LOW)
    spread = jnp.maximum(outside(has_row, row_sum), outside(has_col, col_sum))

    @pl.when(spread > 0.0)
    def _():
        row_ref[...] = jnp.full(row_ref.shape, LOW, F32)
        col_ref[...] = jnp.full(col_ref.shape, LOW, F32)

        def merge(values, ref, at):
            top = jnp.max(values, axis=0, keepdims=True)
            here = top + jnp.log(jnp.sum(jnp.exp(values - top), axis=0, keepdims=True))
            old = ref[pl.ds(at, 1), :]
            peak = jnp.maximum(here, old)
            ref[pl.ds(at, 1), :] = peak + jnp.log(jnp.exp(here - peak) + jnp.exp(old - peak))

        def careful(e, _):
            code = edge_ref[0, e]
            s, p = code // TARGETS, code % TARGETS
            value = SHARP * scores(s, p)
            merge(value, row_ref, s)
            merge(value.T, col_ref, p)
            return 0

        lax.fori_loop(0, count, careful, 0)


def tiles(edges, src, turned, has_row, has_col):
    vmem = pl.BlockSpec(memory_space=pltpu.VMEM)
    shape = jax.ShapeDtypeStruct
    return pl.pallas_call(
        tiles_kernel,
        out_shape=(shape((SOURCES, YS * 128), F32), shape((TARGETS, 256), F32)),
        in_specs=[vmem] * 5,
        out_specs=(vmem, vmem),
        scratch_shapes=[
            pltpu.SMEM((8, LIST), I32),
            pltpu.VMEM((SOURCES + 1, 8, YS * 128), F32),
            pltpu.VMEM((TARGETS, 8, 256), F32),
            pltpu.SemaphoreType.DMA,
        ],
        compiler_params=pltpu.CompilerParams(vmem_limit_bytes=32 * 2**20),
        name="tiles",
    )(edges, src, turned, has_row, has_col)


def log_sum(parts):
    top = functools.reduce(jnp.maximum, parts)
    return top + jnp.log(sum(jnp.exp(part - top) for part in parts))


def settle_kernel(row, col, src_base, tgt_base, kept_pot, src_out, tgt_out,
                  row_y, row_x, row_k, col_k, col_z, wide, row_mid, row_end, col_mid,
                  send_sem, recv_sem):
    z, x, k, y = place()
    turn = lambda at, by, n: lax.rem(at + by, n)
    mate = device(z, x, 1 - k, y)
    xs = [device(z, turn(x, d, XS), k, y) for d in range(1, XS)]
    ys = [device(z, x, k, turn(y, d, YS)) for d in range(1, YS)]
    zs = [device(turn(z, d, ZS), x, k, y) for d in range(1, ZS)]
    barrier = pltpu.get_barrier_semaphore()
    everyone = [mate] + xs + ys + zs
    for other in everyone:
        pl.semaphore_signal(barrier, inc=1, device_id=other, device_id_type=MESH)
    pl.semaphore_wait(barrier, len(everyone))
    used = [0]

    def send(src_ref, dst_ref, to):
        m = used[0]
        used[0] += 1
        copy = pltpu.make_async_remote_copy(
            src_ref=src_ref, dst_ref=dst_ref, send_sem=send_sem.at[m], recv_sem=recv_sem.at[m],
            device_id=to, device_id_type=MESH)
        copy.start()
        return copy

    first = [send(row.at[:, pl.ds(pl.multiple_of(turn(y, d, YS) * 128, 128), 128)], row_y.at[d - 1], ys[d - 1])
             for d in range(1, YS)]
    first.append(send(col.at[:, 1 - k], col_k, mate))
    own_row = row[:, pl.ds(pl.multiple_of(y * 128, 128), 128)]
    for copy in first:
        copy.wait_recv()
    row_mid[...] = log_sum([own_row] + [row_y[d] for d in range(YS - 1)]).reshape(row_mid.shape)
    col_mid[...] = log_sum([col[:, k], col_k[...]])

    second = [send(row_mid.at[turn(x, d, XS)], row_x.at[d - 1], xs[d - 1]) for d in range(1, XS)]
    second += [send(col_mid.at[turn(z, d, ZS)], col_z.at[d - 1], zs[d - 1]) for d in range(1, ZS)]
    for copy in second:
        copy.wait_recv()
    row_end[...] = log_sum([row_mid[x]] + [row_x[d] for d in range(XS - 1)])
    total = log_sum([col_mid[z]] + [col_z[d] for d in range(ZS - 1)])
    result = jnp.where(total > 0.5 * LOW, -0.25 * total + tgt_base[...], kept_pot[...])
    wide[y] = result

    third = [send(row_end.at[1 - k], row_k, mate)]
    third += [send(wide.at[y], wide.at[y], ys[d - 1]) for d in range(1, YS)]
    third[0].wait_recv()
    halves = row_end[k], row_k[...]
    base = src_base[...]
    src_out[:, 0:128] = base[:, 0:128] - 0.25 * jnp.where(k == 0, halves[0], halves[1])
    src_out[:, 128:256] = base[:, 128:256] - 0.25 * jnp.where(k == 0, halves[1], halves[0])
    for d in range(1, YS):
        m = used[0] - YS + d
        pltpu.make_async_remote_copy(
            src_ref=wide.at[turn(y, YS - d, YS)], dst_ref=wide.at[turn(y, YS - d, YS)],
            send_sem=send_sem.at[m], recv_sem=recv_sem.at[m],
            device_id=mate, device_id_type=MESH).wait_recv()
    for at in range(YS):
        tgt_out[:, at * 256:(at + 1) * 256] = wide[at]
    for copy in first + second + third:
        copy.wait_send()


def settle(row, col, src_base, tgt_base, kept_pot):
    vmem = pl.BlockSpec(memory_space=pltpu.VMEM)
    shape = jax.ShapeDtypeStruct
    return pl.pallas_call(
        settle_kernel,
        out_shape=(shape((PER, 256), F32), shape((PER, 1024), F32)),
        in_specs=[vmem] * 5,
        out_specs=(vmem, vmem),
        scratch_shapes=[
            pltpu.VMEM((YS - 1, SOURCES, 128), F32),
            pltpu.VMEM((XS - 1, 2, PER, 128), F32),
            pltpu.VMEM((PER, 128), F32),
            pltpu.VMEM((ZS, PER, 256), F32),
            pltpu.VMEM((ZS - 1, PER, 256), F32),
            pltpu.VMEM((YS, PER, 256), F32),
            pltpu.VMEM((XS, 2, PER, 128), F32),
            pltpu.VMEM((2, PER, 128), F32),
            pltpu.VMEM((ZS, PER, 256), F32),
            pltpu.SemaphoreType.DMA((24,)),
            pltpu.SemaphoreType.DMA((24,)),
        ],
        compiler_params=pltpu.CompilerParams(
            collective_id=1, has_side_effects=True, vmem_limit_bytes=32 * 2**20),
        name="settle",
    )(row, col.reshape(ZS, 2, PER, 256), src_base, tgt_base, kept_pot)


def local(sp, tp, f, g, kept, counts, home):
    src, turned, edges, has_row, has_col, src_base, tgt_base, kept_pot = collect(
        sp, tp, f, g, kept, counts.reshape(1, -1), home.reshape(1, -1))
    row, col = tiles(edges, src, turned, has_row, has_col)
    return settle(row, col, src_base, tgt_base, kept_pot)


def solution(mesh):
    placed = (
        P("clusters", None, "tiles"),
        P("clusters", None, None),
        P("clusters", "tiles"),
        P("clusters", None),
        P(),
        P(),
        P(),
    )
    return jax.shard_map(
        local,
        mesh=mesh,
        in_specs=placed,
        out_specs=(P("clusters", "tiles"), P("clusters", None)),
        check_vma=False,
    )
```

```python
import functools

import jax
import jax.numpy as jnp
from jax import lax
from jax.experimental import pallas as pl
from jax.experimental.pallas import tpu as pltpu
from jax.sharding import PartitionSpec as P

MESH = pl.DeviceIdType.MESH
ZS, XS, YS = 8, 4, 4
PER = 8
SHARP = 4.0
EXP2_SCALE = 5.770780163555854
LOW = -1e30
SOURCES, TARGETS = XS * 2 * PER, ZS * 2 * PER
LIST = 256
CHUNK = 2
EARLY = 1
WIDE, SLIM = 32, 8
F32, BF16, I32 = jnp.float32, jnp.bfloat16, jnp.int32


def place():
    c, y = lax.axis_index("clusters"), lax.axis_index("tiles")
    return c // 8, (c // 2) % 4, c % 2, y


def device(z, x, k, y):
    return (z * 8 + x * 2 + k, y)


def iota(shape, dim):
    return lax.broadcasted_iota(I32, shape, dim)


def widen(points, potential, out):
    values = points.astype(F32)
    half_norm = 0.5 * jnp.sum(values * values, axis=0)
    term = potential - half_norm
    high = term.astype(BF16).astype(F32)
    low = (term - high).astype(BF16).astype(F32)
    full = jnp.concatenate([values, high[None], low[None]], axis=0)
    out(jnp.swapaxes(full, 0, 1).astype(BF16))
    return high + low + half_norm


def edge_list(z, x, kept, counts, home, edges_ref, has_row_ref, has_col_ref):
    lane = iota((SOURCES, 512), 1)
    row = iota((SOURCES, 512), 0)
    mine = lane == row + z * SOURCES
    count = jnp.sum(jnp.where(mine, counts[...].astype(F32), 0.0), axis=1, keepdims=True)
    names = kept[...].astype(F32)
    lane = lane.astype(F32)
    homes = home[...].astype(F32)
    own_row = iota((SOURCES, 1), 0)
    codes, marks, before, total = [], [], [], jnp.zeros((SOURCES, 1), F32)
    for k in range(12):
        name = jnp.sum(jnp.where(mine, names[k:k + 1], 0.0), axis=1, keepdims=True)
        at = jnp.sum(jnp.where(name == lane, homes, 0.0), axis=1, keepdims=True).astype(I32)
        mark = jnp.where((count > float(k)) & (((at >> 4) & 3) == x), 1.0, 0.0)
        codes.append((own_row * TARGETS + ((at >> 6) << 4) + (at & 15) + 1).astype(F32))
        marks.append(mark)
        before.append(total)
        total = total + mark
    square_row, square_lane = iota((SOURCES, SOURCES), 0), iota((SOURCES, SOURCES), 1)
    across = jnp.sum(jnp.where(square_row == square_lane, total, 0.0), axis=0, keepdims=True)
    ahead = jnp.sum(jnp.where(square_lane < square_row, across, 0.0), axis=1, keepdims=True)
    slot = iota((SOURCES, LIST), 1).astype(F32)
    filled = jnp.zeros((SOURCES, LIST), F32)
    for code, mark, prior in zip(codes, marks, before):
        filled = filled + jnp.where((slot == ahead + prior) & (mark > 0.0), code, 0.0)
    listed = jnp.sum(filled, axis=0, keepdims=True)
    number = jnp.sum(total, axis=0, keepdims=True)
    chosen = jnp.where(listed > 0.0, listed - 1.0, float(SOURCES * TARGETS)).astype(I32)
    edges_ref[...] = jnp.where(iota((8, LIST), 0) == 0, chosen, number.astype(I32))
    has_row_ref[...] = jnp.broadcast_to(jnp.where(total > 0.0, 1.0, 0.0), has_row_ref.shape)
    named = (iota((TARGETS, LIST), 0) == (chosen & (TARGETS - 1))) & (listed > 0.0)
    has_col_ref[...] = jnp.broadcast_to(
        jnp.max(jnp.where(named, 1.0, 0.0), axis=1, keepdims=True), has_col_ref.shape)


def idle_kernel(out):
    out[...] = jnp.where(iota(out.shape, 0) == 30, LOW, 0.0)


def idle_source():
    return pl.pallas_call(
        idle_kernel,
        out_shape=jax.ShapeDtypeStruct((32, 128), F32),
        out_specs=pl.BlockSpec(memory_space=pltpu.VMEM),
        name="idle",
        cost_estimate=pl.CostEstimate(flops=10**10, bytes_accessed=10**7, transcendentals=0),
    )()


def collect_kernel(idle, sp, tp, f, g, kept, counts, home,
                   src, turned, edges_ref, has_row_ref, has_col_ref, src_base, tgt_base, kept_pot,
                   spare, tgt, send_sem, recv_sem):
    z, x, k, y = place()
    step = lambda at, by, n: lax.rem(at + (by + n), n)

    mate = device(z, x, 1 - k, y)
    xn = {d: device(z, step(x, d, XS), k, y) for d in (1, -1, 2)}
    yn = {d: device(z, x, k, step(y, d, YS)) for d in (1, -1, 2)}
    zn = {d: device(step(z, d, ZS), x, k, y) for d in (1, -1)}

    barrier = pltpu.get_barrier_semaphore()
    for other in (mate, *xn.values(), *yn.values(), *zn.values()):
        pl.semaphore_signal(barrier, inc=1, device_id=other, device_id_type=MESH)

    numbers = {}
    pending = []

    def descriptor(key, ref, to):
        m = numbers.setdefault(key, len(numbers))
        return pltpu.make_async_remote_copy(
            src_ref=ref, dst_ref=ref, send_sem=send_sem.at[m], recv_sem=recv_sem.at[m],
            device_id=to, device_id_type=MESH)

    def send(key, ref, to):
        copy = descriptor(key, ref, to)
        copy.start()
        pending.append(copy)

    def arrive(key, ref):
        descriptor(key, ref, mate).wait_recv()

    def src_block(dx, dy, q, lo=0, n=PER):
        return src.at[step(y, dy, YS), pl.ds(step(x, dx, XS) * 16 + q * 8 + lo, n)]


    def put_target(block):
        tgt[z, k] = block

    quarter = pl.ds(pl.multiple_of(y * 256, 256), 256)
    tgt_base[...] = widen(tp[:, :, quarter], g[:, quarter], put_target)
    kept_pot[...] = g[:, quarter]
    pl.semaphore_wait(barrier, 9)

    def tgt_chunk(dz, c, core):
        return tgt.at[step(z, dz, ZS), core, pl.ds(c * CHUNK, CHUNK)]

    wide_id = iota((32, 256), 0)
    tail_id = iota((16, 256), 0)

    def turn(dz, c, core):
        zz = step(z, dz, ZS)

        def one(i, _):
            block = tgt[zz, core, c * CHUNK + i].astype(F32)
            top = jnp.where(wide_id < 30, block, 1.0)
            low = jnp.where(tail_id >= 14, block[16:32], 0.0)
            turned[zz * 16 + core * 8 + c * CHUNK + i] = jnp.concatenate([top, low], axis=0).T.astype(BF16)
            return 0

        lax.fori_loop(0, CHUNK, one, 0, unroll=CHUNK)

    def take_target(d, dz, c, forward):
        arrive(("z", d, dz + d, c), tgt_chunk(dz, c, k))
        for e in forward:
            send(("z", e, dz, c), tgt_chunk(dz, c, k), zn[e])
        send(("m", dz, c), tgt_chunk(dz, c, k), mate)

    def take_mate(dz, c):
        arrive(("m", dz, c), tgt_chunk(dz, c, 1 - k))
        turn(dz, c, 1 - k)

    def off(q, first, second):
        return (first, second) if q == 0 else (second, first)

    near = {0: (xn, yn), 1: (yn, xn)}

    def first_out(q):
        for d in (1, -1, 2):
            send(("a", q, d), src_block(0, 0, q), near[q][0][d])

    def first_in(q, d):
        arrive(("a", q, d), src_block(*off(q, -d, 0), q))

    def second_out(q, e):
        for d in (1, -1) if e != 2 else (2, 1, -1):
            send(("b", q, e, d), src_block(*off(q, e, 0), q), near[q][1][d])

    def second_in(q, e):
        for d in (1, -1):
            dx, dy = off(q, e, -d)
            arrive(("b", q, e, d), src_block(dx, dy, q))
            if e != 2:
                send(("bf", q, e, d), src_block(dx, dy, q, 0 if d == 1 else 4, 4), near[q][1][d])

    def second_far(q, e):
        dx, dy = off(q, e, 2)
        if e == 2:
            arrive(("b", q, e, 2), src_block(dx, dy, q))
            return
        for d in (1, -1):
            arrive(("bf", q, e, d), src_block(dx, dy, q, 0 if d == 1 else 4, 4))

    def put_source(block):
        halves = block[:, :, 0:128], block[:, :, 128:256]
        src[y, pl.ds(x * 16 + k * 8, PER)] = jnp.where(k == 0, halves[0], halves[1])
        spare[...] = jnp.where(k == 0, halves[1], halves[0])

    chunks = PER // CHUNK
    up = tuple(range(chunks))
    down = up[::-1]

    for c, e in zip(up, down):
        send(("z", 1, 0, c), tgt_chunk(0, c, k), zn[1])
        send(("z", -1, 0, e), tgt_chunk(0, e, k), zn[-1])
    src_base[...] = widen(sp[...], f[...], put_source)
    cross = pltpu.make_async_remote_copy(
        src_ref=spare, dst_ref=src.at[y, pl.ds(x * 16 + k * 8, PER)],
        send_sem=send_sem.at[numbers.setdefault("cross", len(numbers))],
        recv_sem=recv_sem.at[numbers["cross"]], device_id=mate, device_id_type=MESH)
    cross.start()
    pending.append(cross)

    pltpu.make_async_remote_copy(
        src_ref=spare, dst_ref=src.at[y, pl.ds(x * 16 + (1 - k) * 8, PER)],
        send_sem=send_sem.at[numbers["cross"]], recv_sem=recv_sem.at[numbers["cross"]],
        device_id=mate, device_id_type=MESH).wait_recv()
    for q in (0, 1):
        first_out(q)
    for q in (0, 1):
        second_out(q, 0)
    for c in up:
        send(("m", 0, c), tgt_chunk(0, c, k), mate)

    waiting = [(turn, 0, c, k) for c in up] + [(take_mate, 0, c) for c in up]

    def work(n):
        for job in waiting[:n]:
            job[0](*job[1:])
        del waiting[:n]

    def targets_in(hop, c, e):
        for d, dz, at in ((1, -hop, c), (-1, hop, e)):
            if hop < 4 or at in (up[:chunks // 2] if d == 1 else up[chunks // 2:]):
                on = hop < 3 or (hop == 3 and at in (up[:chunks // 2] if d == 1 else up[chunks // 2:]))
                take_target(d, dz, at, (d,) if on else ())
                waiting.append((turn, dz, at, k))
                waiting.append((take_mate, dz, at))

    def sources_in(hop):
        for q in (0, 1):
            if hop == 1:
                for d in (1, -1):
                    first_in(q, d)
                    second_out(q, -d)
            elif hop == 2:
                second_in(q, 0)
                first_in(q, 2)
                second_out(q, 2)
            elif hop == 3:
                second_in(q, 1)
                second_in(q, -1)
            else:
                second_in(q, 2)

    for hop in range(1, 5):
        for i, (c, e) in enumerate(zip(up, down)):
            targets_in(hop, c, e)
            if i == EARLY:
                sources_in(hop)
            if hop == 1 and i == chunks - 1:
                edge_list(z, x, kept, counts, home, edges_ref, has_row_ref, has_col_ref)
                for at in range(YS):
                    src[at, SOURCES] = idle[...].astype(BF16)
            work(4)
    work(len(waiting))
    for q in (0, 1):
        for e in (0, -1, 1, 2):
            second_far(q, e)
    for copy in pending:
        copy.wait_send()


MESSAGES = 128


def collect(sp, tp, f, g, kept, counts, home):
    vmem = pl.BlockSpec(memory_space=pltpu.VMEM)
    shape = jax.ShapeDtypeStruct
    return pl.pallas_call(
        collect_kernel,
        out_shape=(
            shape((YS, SOURCES + 1, 32, 128), BF16),
            shape((TARGETS, 256, 48), BF16),
            shape((8, LIST), I32),
            shape((SOURCES, 128), F32),
            shape((TARGETS, 128), F32),
            shape((PER, 256), F32),
            shape((PER, 256), F32),
            shape((PER, 256), F32),
        ),
        in_specs=[vmem] * 8,
        out_specs=(vmem,) * 8,
        scratch_shapes=[
            pltpu.VMEM((PER, 32, 128), BF16),
            pltpu.VMEM((ZS, 2, PER, 32, 256), BF16),
            pltpu.SemaphoreType.DMA((MESSAGES,)),
            pltpu.SemaphoreType.DMA((MESSAGES,)),
        ],
        compiler_params=pltpu.CompilerParams(
            collective_id=0, has_side_effects=True, vmem_limit_bytes=32 * 2**20),
        name="collect",
    )(idle_source(), sp, tp, f, g, kept, counts, home)


def tiles_kernel(edge_vmem, src, turned, has_row_ref, has_col_ref, row_ref, col_ref,
                 edge_ref, row_acc, col_acc, edge_sem):
    load = pltpu.make_async_copy(edge_vmem, edge_ref, edge_sem)
    load.start()
    width = turned.shape[1]
    tail = jnp.where(iota((16, YS * 128), 0) >= 14, 1.0, 0.0).astype(BF16)
    row_acc[...] = jnp.zeros(row_acc.shape, F32)
    col_acc[...] = jnp.zeros(col_acc.shape, F32)
    load.wait()
    count = edge_ref[1, 0]

    def scores(s, p):
        cells = jnp.concatenate([src[at, s] for at in range(YS)], axis=1)
        right = jnp.concatenate([cells, tail], axis=0)
        return jnp.dot(turned[p], right, preferred_element_type=F32)

    def edge(at):
        code = edge_ref[0, at]
        s, p = code // TARGETS, code % TARGETS
        e = jnp.exp2(scores(s, p) * EXP2_SCALE)
        q = (e[:, 0:128] + e[:, 128:256]) + (e[:, 256:384] + e[:, 384:512])
        row_acc[s] += e.reshape(width // 8, 8, YS * 128).sum(axis=0)
        col_acc[p] += q.T.reshape(16, 8, width).sum(axis=0)

    def step(start, size):
        def run(it, _):
            for u in range(size):
                edge(start + it * size + u)
            return 0

        return run

    wide = (count + SLIM - 1) // WIDE
    lax.fori_loop(0, wide, step(0, WIDE), 0)
    rest = jnp.maximum(count - wide * WIDE, 0)
    lax.fori_loop(0, (rest + SLIM - 1) // SLIM, step(wide * WIDE, SLIM), 0)

    row_sum = jnp.sum(row_acc[0:SOURCES], axis=1)
    col_sum = jnp.sum(col_acc[...], axis=1)
    has_row = has_row_ref[:, 0:1] > 0.0
    has_col = has_col_ref[:, 0:1] > 0.0

    def outside(has, total):
        good = (total >= 2.0**-90) & (total <= 2.0**120)
        return jnp.max(jnp.where(has & jnp.logical_not(good), 1.0, 0.0))

    row_ref[...] = jnp.where(has_row, jnp.log(jnp.where(has_row, row_sum, 1.0)), LOW)
    col_ref[...] = jnp.where(has_col, jnp.log(jnp.where(has_col, col_sum, 1.0)), LOW)
    spread = jnp.maximum(outside(has_row, row_sum), outside(has_col, col_sum))

    @pl.when(spread > 0.0)
    def _():
        row_ref[...] = jnp.full(row_ref.shape, LOW, F32)
        col_ref[...] = jnp.full(col_ref.shape, LOW, F32)

        def merge(values, ref, at):
            top = jnp.max(values, axis=0, keepdims=True)
            here = top + jnp.log(jnp.sum(jnp.exp(values - top), axis=0, keepdims=True))
            old = ref[pl.ds(at, 1), :]
            peak = jnp.maximum(here, old)
            ref[pl.ds(at, 1), :] = peak + jnp.log(jnp.exp(here - peak) + jnp.exp(old - peak))

        def careful(e, _):
            code = edge_ref[0, e]
            s, p = code // TARGETS, code % TARGETS
            value = SHARP * scores(s, p)
            merge(value, row_ref, s)
            merge(value.T, col_ref, p)
            return 0

        lax.fori_loop(0, count, careful, 0)


def tiles(edges, src, turned, has_row, has_col):
    vmem = pl.BlockSpec(memory_space=pltpu.VMEM)
    shape = jax.ShapeDtypeStruct
    return pl.pallas_call(
        tiles_kernel,
        out_shape=(shape((SOURCES, YS * 128), F32), shape((TARGETS, 256), F32)),
        in_specs=[vmem] * 5,
        out_specs=(vmem, vmem),
        scratch_shapes=[
            pltpu.SMEM((8, LIST), I32),
            pltpu.VMEM((SOURCES + 1, 8, YS * 128), F32),
            pltpu.VMEM((TARGETS, 8, 256), F32),
            pltpu.SemaphoreType.DMA,
        ],
        compiler_params=pltpu.CompilerParams(vmem_limit_bytes=32 * 2**20),
        name="tiles",
    )(edges, src, turned, has_row, has_col)


def log_sum(parts):
    top = functools.reduce(jnp.maximum, parts)
    return top + jnp.log(sum(jnp.exp(part - top) for part in parts))


def settle_kernel(row, col, src_base, tgt_base, kept_pot, src_out, tgt_out,
                  row_y, row_x, col_z, wide, row_mid, send_sem, recv_sem):
    z, x, k, y = place()
    turn = lambda at, by, n: lax.rem(at + by, n)
    row_moves = [(dk, dy) for dk in (1, 0) for dy in (2, 1, 3, 0) if dk or dy]
    col_moves = [(dz, dk) for dz in (4, 3, 5, 2, 6, 1, 7, 0) for dk in (1, 0) if dz or dk]
    core = lambda dk: turn(k, dk, 2)
    xs = [device(z, turn(x, d, XS), k, y) for d in (2, 1, 3)]
    ys = [device(z, x, k, turn(y, d, YS)) for d in (2, 1, 3)]
    row_to = [device(z, x, core(dk), turn(y, dy, YS)) for dk, dy in row_moves]
    col_to = [device(turn(z, dz, ZS), x, core(dk), y) for dz, dk in col_moves]
    barrier = pltpu.get_barrier_semaphore()
    everyone = [to for to, (dz, dk) in zip(col_to, col_moves) if dz] + row_to + xs
    for other in everyone:
        pl.semaphore_signal(barrier, inc=1, device_id=other, device_id_type=MESH)
    pl.semaphore_wait(barrier, len(everyone))
    used = [0]

    def send(src_ref, dst_ref, to):
        m = used[0]
        used[0] += 1
        copy = pltpu.make_async_remote_copy(
            src_ref=src_ref, dst_ref=dst_ref, send_sem=send_sem.at[m], recv_sem=recv_sem.at[m],
            device_id=to, device_id_type=MESH)
        copy.start()
        return copy

    def quarter(at):
        return pl.ds(pl.multiple_of(at * 128, 128), 128)

    cols = [send(col.at[turn(z, dz, ZS), core(dk)], col_z.at[i], col_to[i]) for i, (dz, dk) in enumerate(col_moves)]
    rows = [send(row.at[:, core(dk), :, quarter(turn(y, dy, YS))], row_y.at[i], row_to[i])
            for i, (dk, dy) in enumerate(row_moves)]
    for copy in rows:
        copy.wait_recv()
    own = row[:, k, :, quarter(y)]
    row_mid[:, k] = log_sum([own] + [row_y[i] for i, (dk, _) in enumerate(row_moves) if dk == 0])
    row_mid[:, 1 - k] = log_sum([row_y[i] for i, (dk, _) in enumerate(row_moves) if dk == 1])

    across = [send(row_mid.at[turn(x, d, XS)], row_x.at[i], xs[i]) for i, d in enumerate((2, 1, 3))]
    for copy in cols:
        copy.wait_recv()
    total = log_sum([col[z, k]] + [col_z[i] for i in range(len(col_moves))])
    wide[y] = jnp.where(total > 0.5 * LOW, -0.25 * total + tgt_base[...], kept_pot[...])
    shares = [send(wide.at[y], wide.at[y], ys[i]) for i in range(YS - 1)]
    for copy in across:
        copy.wait_recv()
    ends = log_sum([row_mid[x]] + [row_x[i] for i in range(XS - 1)])
    src_out[:, 0:128] = src_base[:, 0:128] - 0.25 * ends[0]
    src_out[:, 128:256] = src_base[:, 128:256] - 0.25 * ends[1]
    for i, d in enumerate((2, 1, 3)):
        m = used[0] - (YS - 1) + i
        came = wide.at[turn(y, YS - d, YS)]
        pltpu.make_async_remote_copy(
            src_ref=came, dst_ref=came, send_sem=send_sem.at[m], recv_sem=recv_sem.at[m],
            device_id=ys[i], device_id_type=MESH).wait_recv()
    for at in range(YS):
        tgt_out[:, at * 256:(at + 1) * 256] = wide[at]
    for copy in cols + rows + across + shares:
        copy.wait_send()


def settle(row, col, src_base, tgt_base, kept_pot):
    vmem = pl.BlockSpec(memory_space=pltpu.VMEM)
    shape = jax.ShapeDtypeStruct
    return pl.pallas_call(
        settle_kernel,
        out_shape=(shape((PER, 256), F32), shape((PER, 1024), F32)),
        in_specs=[vmem] * 5,
        out_specs=(vmem, vmem),
        scratch_shapes=[
            pltpu.VMEM((7, XS, PER, 128), F32),
            pltpu.VMEM((XS - 1, 2, PER, 128), F32),
            pltpu.VMEM((15, PER, 256), F32),
            pltpu.VMEM((YS, PER, 256), F32),
            pltpu.VMEM((XS, 2, PER, 128), F32),
            pltpu.SemaphoreType.DMA((32,)),
            pltpu.SemaphoreType.DMA((32,)),
        ],
        compiler_params=pltpu.CompilerParams(
            collective_id=1, has_side_effects=True, vmem_limit_bytes=32 * 2**20),
        name="settle",
    )(row.reshape(XS, 2, PER, YS * 128), col.reshape(ZS, 2, PER, 256), src_base, tgt_base, kept_pot)


def local(sp, tp, f, g, kept, counts, home):
    src, turned, edges, has_row, has_col, src_base, tgt_base, kept_pot = collect(
        jnp.swapaxes(sp, 0, 1), jnp.swapaxes(tp, 0, 1), f, g, kept.T, counts.reshape(1, -1), home.reshape(1, -1))
    row, col = tiles(edges, src, turned, has_row, has_col)
    return settle(row, col, src_base, tgt_base, kept_pot)


def solution(mesh):
    placed = (
        P("clusters", None, "tiles"),
        P("clusters", None, None),
        P("clusters", "tiles"),
        P("clusters", None),
        P(),
        P(),
        P(),
    )
    return jax.shard_map(
        local,
        mesh=mesh,
        in_specs=placed,
        out_specs=(P("clusters", "tiles"), P("clusters", None)),
        check_vma=False,
    )
```

```python
import functools

import jax
import jax.numpy as jnp
from jax import lax
from jax.experimental import pallas as pl
from jax.experimental.pallas import tpu as pltpu
from jax.sharding import PartitionSpec as P

MESH = pl.DeviceIdType.MESH
ZS, XS, YS = 8, 4, 4
PER = 8
SHARP = 4.0
EXP2_SCALE = 5.770780163555854
LOW = -1e30
SOURCES, TARGETS = XS * 2 * PER, ZS * 2 * PER
LIST = 256
CHUNK = 2
EARLY = 1
WIDE, SLIM = 32, 8
F32, BF16, I32 = jnp.float32, jnp.bfloat16, jnp.int32


def place():
    c, y = lax.axis_index("clusters"), lax.axis_index("tiles")
    return c // 8, (c // 2) % 4, c % 2, y


def device(z, x, k, y):
    return (z * 8 + x * 2 + k, y)


def iota(shape, dim):
    return lax.broadcasted_iota(I32, shape, dim)


def widen(points, potential, out):
    values = points.astype(F32)
    half_norm = 0.5 * jnp.sum(values * values, axis=0)
    term = potential - half_norm
    high = term.astype(BF16).astype(F32)
    low = (term - high).astype(BF16).astype(F32)
    full = jnp.concatenate([values, high[None], low[None]], axis=0)
    out(jnp.swapaxes(full, 0, 1).astype(BF16))
    return high + low + half_norm


def edge_list(z, x, kept, counts, home, edges_ref, has_row_ref, has_col_ref, no_row_ref, no_col_ref):
    lane = iota((SOURCES, 512), 1)
    row = iota((SOURCES, 512), 0)
    mine = lane == row + z * SOURCES
    count = jnp.sum(jnp.where(mine, counts[...].astype(F32), 0.0), axis=1, keepdims=True)
    names = kept[...].astype(F32)
    lane = lane.astype(F32)
    homes = home[...].astype(F32)
    own_row = iota((SOURCES, 1), 0)
    codes, marks, before, total = [], [], [], jnp.zeros((SOURCES, 1), F32)
    for k in range(12):
        name = jnp.sum(jnp.where(mine, names[k:k + 1], 0.0), axis=1, keepdims=True)
        at = jnp.sum(jnp.where(name == lane, homes, 0.0), axis=1, keepdims=True).astype(I32)
        mark = jnp.where((count > float(k)) & (((at >> 4) & 3) == x), 1.0, 0.0)
        codes.append((own_row * TARGETS + ((at >> 6) << 4) + (at & 15) + 1).astype(F32))
        marks.append(mark)
        before.append(total)
        total = total + mark
    square_row, square_lane = iota((SOURCES, SOURCES), 0), iota((SOURCES, SOURCES), 1)
    across = jnp.sum(jnp.where(square_row == square_lane, total, 0.0), axis=0, keepdims=True)
    ahead = jnp.sum(jnp.where(square_lane < square_row, across, 0.0), axis=1, keepdims=True)
    slot = iota((SOURCES, LIST), 1).astype(F32)
    filled = jnp.zeros((SOURCES, LIST), F32)
    for code, mark, prior in zip(codes, marks, before):
        filled = filled + jnp.where((slot == ahead + prior) & (mark > 0.0), code, 0.0)
    listed = jnp.sum(filled, axis=0, keepdims=True)
    number = jnp.sum(total, axis=0, keepdims=True)
    chosen = jnp.where(listed > 0.0, listed - 1.0, float(SOURCES * TARGETS)).astype(I32)
    edges_ref[...] = jnp.where(iota((8, LIST), 0) == 0, chosen, number.astype(I32))
    has_row = jnp.where(total > 0.0, 1.0, 0.0)
    named = (iota((TARGETS, LIST), 0) == (chosen & (TARGETS - 1))) & (listed > 0.0)
    has_col = jnp.max(jnp.where(named, 1.0, 0.0), axis=1, keepdims=True)
    for has, has_ref, no_ref in ((has_row, has_row_ref, no_row_ref), (has_col, has_col_ref, no_col_ref)):
        has_ref[...] = jnp.broadcast_to(has, has_ref.shape)
        no_ref[...] = jnp.broadcast_to((1.0 - has_ref[...])[:, None, :], no_ref.shape)


def idle_kernel(out):
    out[...] = jnp.where(iota(out.shape, 0) == 30, LOW, 0.0)


def idle_source():
    return pl.pallas_call(
        idle_kernel,
        out_shape=jax.ShapeDtypeStruct((32, 128), F32),
        out_specs=pl.BlockSpec(memory_space=pltpu.VMEM),
        name="idle",
        cost_estimate=pl.CostEstimate(flops=10**10, bytes_accessed=3 * 10**7, transcendentals=0),
    )()


def collect_kernel(idle, sp, tp, f, g, kept, counts, home,
                   src, turned, edges_ref, has_row_ref, has_col_ref, no_row_ref, no_col_ref, src_base, tgt_base, kept_pot,
                   spare, tgt, send_sem, recv_sem):
    z, x, k, y = place()
    step = lambda at, by, n: lax.rem(at + (by + n), n)

    mate = device(z, x, 1 - k, y)
    xn = {d: device(z, step(x, d, XS), k, y) for d in (1, -1, 2)}
    yn = {d: device(z, x, k, step(y, d, YS)) for d in (1, -1, 2)}
    zn = {d: device(step(z, d, ZS), x, k, y) for d in (1, -1)}

    barrier = pltpu.get_barrier_semaphore()
    for other in (mate, *xn.values(), *yn.values(), *zn.values()):
        pl.semaphore_signal(barrier, inc=1, device_id=other, device_id_type=MESH)

    numbers = {}
    pending = []

    def descriptor(key, ref, to):
        m = numbers.setdefault(key, len(numbers))
        return pltpu.make_async_remote_copy(
            src_ref=ref, dst_ref=ref, send_sem=send_sem.at[m], recv_sem=recv_sem.at[m],
            device_id=to, device_id_type=MESH)

    def send(key, ref, to):
        copy = descriptor(key, ref, to)
        copy.start()
        pending.append(copy)

    def arrive(key, ref):
        descriptor(key, ref, mate).wait_recv()

    def src_block(dx, dy, q, lo=0, n=PER):
        return src.at[step(y, dy, YS), pl.ds(step(x, dx, XS) * 16 + q * 8 + lo, n)]


    def put_target(block):
        tgt[z, k] = block

    quarter = pl.ds(pl.multiple_of(y * 256, 256), 256)
    tgt_base[...] = widen(tp[:, :, quarter], g[:, quarter], put_target)
    kept_pot[...] = g[:, quarter]
    pl.semaphore_wait(barrier, 9)

    def tgt_chunk(dz, c, core):
        return tgt.at[step(z, dz, ZS), core, pl.ds(c * CHUNK, CHUNK)]

    wide_id = iota((32, 256), 0)
    tail_id = iota((16, 256), 0)

    def turn(dz, c, core):
        zz = step(z, dz, ZS)

        def one(i, _):
            block = tgt[zz, core, c * CHUNK + i].astype(F32)
            top = jnp.where(wide_id < 30, block, 1.0)
            low = jnp.where(tail_id >= 14, block[16:32], 0.0)
            turned[zz * 16 + core * 8 + c * CHUNK + i] = jnp.concatenate([top, low], axis=0).T.astype(BF16)
            return 0

        lax.fori_loop(0, CHUNK, one, 0, unroll=CHUNK)

    def take_target(d, dz, c, forward):
        arrive(("z", d, dz + d, c), tgt_chunk(dz, c, k))
        for e in forward:
            send(("z", e, dz, c), tgt_chunk(dz, c, k), zn[e])
        send(("m", dz, c), tgt_chunk(dz, c, k), mate)

    def take_mate(dz, c):
        arrive(("m", dz, c), tgt_chunk(dz, c, 1 - k))
        turn(dz, c, 1 - k)

    def off(q, first, second):
        return (first, second) if q == 0 else (second, first)

    near = {0: (xn, yn), 1: (yn, xn)}

    def first_out(q):
        for d in (1, -1, 2):
            send(("a", q, d), src_block(0, 0, q), near[q][0][d])

    def first_in(q, d):
        arrive(("a", q, d), src_block(*off(q, -d, 0), q))

    def second_out(q, e):
        for d in (1, -1) if e != 2 else (2, 1, -1):
            send(("b", q, e, d), src_block(*off(q, e, 0), q), near[q][1][d])

    def second_in(q, e):
        for d in (1, -1):
            dx, dy = off(q, e, -d)
            arrive(("b", q, e, d), src_block(dx, dy, q))
            if e != 2:
                send(("bf", q, e, d), src_block(dx, dy, q, 0 if d == 1 else 4, 4), near[q][1][d])

    def second_far(q, e):
        dx, dy = off(q, e, 2)
        if e == 2:
            arrive(("b", q, e, 2), src_block(dx, dy, q))
            return
        for d in (1, -1):
            arrive(("bf", q, e, d), src_block(dx, dy, q, 0 if d == 1 else 4, 4))

    def put_source(block):
        halves = block[:, :, 0:128], block[:, :, 128:256]
        src[y, pl.ds(x * 16 + k * 8, PER)] = jnp.where(k == 0, halves[0], halves[1])
        spare[...] = jnp.where(k == 0, halves[1], halves[0])

    chunks = PER // CHUNK
    up = tuple(range(chunks))
    down = up[::-1]

    for c, e in zip(up, down):
        send(("z", 1, 0, c), tgt_chunk(0, c, k), zn[1])
        send(("z", -1, 0, e), tgt_chunk(0, e, k), zn[-1])
    src_base[...] = widen(sp[...], f[...], put_source)
    cross = pltpu.make_async_remote_copy(
        src_ref=spare, dst_ref=src.at[y, pl.ds(x * 16 + k * 8, PER)],
        send_sem=send_sem.at[numbers.setdefault("cross", len(numbers))],
        recv_sem=recv_sem.at[numbers["cross"]], device_id=mate, device_id_type=MESH)
    cross.start()
    pending.append(cross)

    pltpu.make_async_remote_copy(
        src_ref=spare, dst_ref=src.at[y, pl.ds(x * 16 + (1 - k) * 8, PER)],
        send_sem=send_sem.at[numbers["cross"]], recv_sem=recv_sem.at[numbers["cross"]],
        device_id=mate, device_id_type=MESH).wait_recv()
    for q in (0, 1):
        first_out(q)
    for q in (0, 1):
        second_out(q, 0)
    for c in up:
        send(("m", 0, c), tgt_chunk(0, c, k), mate)

    waiting = [(turn, 0, c, k) for c in up] + [(take_mate, 0, c) for c in up]

    def work(n):
        for job in waiting[:n]:
            job[0](*job[1:])
        del waiting[:n]

    def targets_in(hop, c, e):
        for d, dz, at in ((1, -hop, c), (-1, hop, e)):
            if hop < 4 or at in (up[:chunks // 2] if d == 1 else up[chunks // 2:]):
                on = hop < 3 or (hop == 3 and at in (up[:chunks // 2] if d == 1 else up[chunks // 2:]))
                take_target(d, dz, at, (d,) if on else ())
                waiting.append((turn, dz, at, k))
                waiting.append((take_mate, dz, at))

    def sources_in(hop):
        for q in (0, 1):
            if hop == 1:
                for d in (1, -1):
                    first_in(q, d)
                    second_out(q, -d)
            elif hop == 2:
                second_in(q, 0)
                first_in(q, 2)
                second_out(q, 2)
            elif hop == 3:
                second_in(q, 1)
                second_in(q, -1)
            else:
                second_in(q, 2)

    for hop in range(1, 5):
        for i, (c, e) in enumerate(zip(up, down)):
            targets_in(hop, c, e)
            if i == EARLY:
                sources_in(hop)
            if hop == 1 and i == chunks - 1:
                edge_list(z, x, kept, counts, home, edges_ref, has_row_ref, has_col_ref, no_row_ref, no_col_ref)
                for at in range(YS):
                    src[at, SOURCES] = idle[...].astype(BF16)
            work(4)
    work(len(waiting))
    for q in (0, 1):
        for e in (0, -1, 1, 2):
            second_far(q, e)
    for copy in pending:
        copy.wait_send()


MESSAGES = 128


def collect(sp, tp, f, g, kept, counts, home):
    vmem = pl.BlockSpec(memory_space=pltpu.VMEM)
    shape = jax.ShapeDtypeStruct
    return pl.pallas_call(
        collect_kernel,
        out_shape=(
            shape((YS, SOURCES + 1, 32, 128), BF16),
            shape((TARGETS, 256, 48), BF16),
            shape((8, LIST), I32),
            shape((SOURCES, 128), F32),
            shape((TARGETS, 128), F32),
            shape((SOURCES, 8, 128), F32),
            shape((TARGETS, 8, 128), F32),
            shape((PER, 256), F32),
            shape((PER, 256), F32),
            shape((PER, 256), F32),
        ),
        in_specs=[vmem] * 8,
        out_specs=(vmem,) * 10,
        scratch_shapes=[
            pltpu.VMEM((PER, 32, 128), BF16),
            pltpu.VMEM((ZS, 2, PER, 32, 256), BF16),
            pltpu.SemaphoreType.DMA((MESSAGES,)),
            pltpu.SemaphoreType.DMA((MESSAGES,)),
        ],
        compiler_params=pltpu.CompilerParams(
            collective_id=0, has_side_effects=True, vmem_limit_bytes=32 * 2**20),
        name="collect",
    )(idle_source(), sp, tp, f, g, kept, counts, home)


def tiles_kernel(edge_vmem, src, turned, no_row, no_col, row_acc, col_acc, wild_ref, edge_ref, edge_sem):
    load = pltpu.make_async_copy(edge_vmem, edge_ref, edge_sem)
    load.start()
    width = turned.shape[1]
    tail = jnp.where(iota((16, YS * 128), 0) >= 14, 1.0, 0.0).astype(BF16)
    row_acc[0:SOURCES] = jnp.concatenate([no_row[...]] * YS, axis=2)
    row_acc[SOURCES] = jnp.zeros((8, YS * 128), F32)
    col_acc[...] = jnp.concatenate([no_col[...]] * 2, axis=2)
    load.wait()
    count = edge_ref[1, 0]

    def scores(s, p):
        cells = jnp.concatenate([src[at, s] for at in range(YS)], axis=1)
        right = jnp.concatenate([cells, tail], axis=0)
        return jnp.dot(turned[p], right, preferred_element_type=F32)

    def edge(at):
        code = edge_ref[0, at]
        s, p = code // TARGETS, code % TARGETS
        e = jnp.exp2(scores(s, p) * EXP2_SCALE)
        q = (e[:, 0:128] + e[:, 128:256]) + (e[:, 256:384] + e[:, 384:512])
        row_acc[s] += e.reshape(width // 8, 8, YS * 128).sum(axis=0)
        col_acc[p] += q.T.reshape(16, 8, width).sum(axis=0)

    def step(start, size):
        def run(it, _):
            for u in range(size):
                edge(start + it * size + u)
            return 0

        return run

    wide = (count + SLIM - 1) // WIDE
    lax.fori_loop(0, wide, step(0, WIDE), 0)
    rest = jnp.maximum(count - wide * WIDE, 0)
    lax.fori_loop(0, (rest + SLIM - 1) // SLIM, step(wide * WIDE, SLIM), 0)

    low = jnp.minimum(jnp.min(row_acc[0:SOURCES]), jnp.min(col_acc[...]))
    high = jnp.maximum(jnp.max(row_acc[0:SOURCES]), jnp.max(col_acc[...]))
    wild = jnp.logical_not((low >= 2.0**-90) & (high <= 2.0**116))
    wild_ref[...] = jnp.where(wild, jnp.ones(wild_ref.shape, F32), 0.0)

    @pl.when(wild)
    def _():
        row_acc[...] = jnp.full(row_acc.shape, LOW, F32)
        col_acc[...] = jnp.full(col_acc.shape, LOW, F32)

        def merge(values, ref, at):
            top = jnp.max(values, axis=0, keepdims=True)
            here = top + jnp.log(jnp.sum(jnp.exp(values - top), axis=0, keepdims=True))
            old = ref[at, 0:1, :]
            peak = jnp.maximum(here, old)
            ref[at, 0:1, :] = peak + jnp.log(jnp.exp(here - peak) + jnp.exp(old - peak))

        def careful(e, _):
            code = edge_ref[0, e]
            s, p = code // TARGETS, code % TARGETS
            value = SHARP * scores(s, p)
            merge(value, row_acc, s)
            merge(value.T, col_acc, p)
            return 0

        lax.fori_loop(0, count, careful, 0)


def tiles(edges, src, turned, no_row, no_col):
    vmem = pl.BlockSpec(memory_space=pltpu.VMEM)
    shape = jax.ShapeDtypeStruct
    return pl.pallas_call(
        tiles_kernel,
        out_shape=(
            shape((SOURCES + 1, 8, YS * 128), F32),
            shape((TARGETS, 8, 256), F32),
            shape((8, 128), F32),
        ),
        in_specs=[vmem] * 5,
        out_specs=(vmem,) * 3,
        scratch_shapes=[
            pltpu.SMEM((8, LIST), I32),
            pltpu.SemaphoreType.DMA,
        ],
        compiler_params=pltpu.CompilerParams(vmem_limit_bytes=32 * 2**20),
        name="tiles",
    )(edges, src, turned, no_row, no_col)


def log_sum(parts):
    top = functools.reduce(jnp.maximum, parts)
    return top + jnp.log(sum(jnp.exp(part - top) for part in parts))


def settle_kernel(row_acc, col_acc, wild_ref, has_row, has_col, src_base, tgt_base, kept_pot, src_out, tgt_out,
                  row, col, row_y, row_x, col_z, wide, row_mid, send_sem, recv_sem):
    z, x, k, y = place()
    turn = lambda at, by, n: lax.rem(at + by, n)
    row_moves = [(dk, dy) for dk in (1, 0) for dy in (2, 1, 3, 0) if dk or dy]
    col_moves = [(dz, dk) for dz in (4, 3, 5, 2, 6, 1, 7, 0) for dk in (1, 0) if dz or dk]
    core = lambda dk: turn(k, dk, 2)
    xs = [device(z, turn(x, d, XS), k, y) for d in (2, 1, 3)]
    ys = [device(z, x, k, turn(y, d, YS)) for d in (2, 1, 3)]
    row_to = [device(z, x, core(dk), turn(y, dy, YS)) for dk, dy in row_moves]
    col_to = [device(turn(z, dz, ZS), x, core(dk), y) for dz, dk in col_moves]
    barrier = pltpu.get_barrier_semaphore()
    everyone = [to for to, (dz, dk) in zip(col_to, col_moves) if dz] + row_to + xs
    for other in everyone:
        pl.semaphore_signal(barrier, inc=1, device_id=other, device_id_type=MESH)

    wild = wild_ref[0:1, 0:1] > 0.0

    def logs(acc, has, out):
        has = has[:, 0:1] > 0.0
        total = jnp.where(has, jnp.sum(acc, axis=1), 1.0)
        out[...] = jnp.where(has, jnp.where(wild, acc[:, 0], jnp.log(total)), LOW).reshape(out.shape)

    logs(row_acc[0:SOURCES], has_row, row)
    logs(col_acc[...], has_col, col)
    pl.semaphore_wait(barrier, len(everyone))
    used = [0]

    def send(src_ref, dst_ref, to):
        m = used[0]
        used[0] += 1
        copy = pltpu.make_async_remote_copy(
            src_ref=src_ref, dst_ref=dst_ref, send_sem=send_sem.at[m], recv_sem=recv_sem.at[m],
            device_id=to, device_id_type=MESH)
        copy.start()
        return copy

    def quarter(at):
        return pl.ds(pl.multiple_of(at * 128, 128), 128)

    cols = [send(col.at[turn(z, dz, ZS), core(dk)], col_z.at[i], col_to[i]) for i, (dz, dk) in enumerate(col_moves)]
    rows = [send(row.at[:, core(dk), :, quarter(turn(y, dy, YS))], row_y.at[i], row_to[i])
            for i, (dk, dy) in enumerate(row_moves)]
    for copy in rows:
        copy.wait_recv()
    own = row[:, k, :, quarter(y)]
    row_mid[:, k] = log_sum([own] + [row_y[i] for i, (dk, _) in enumerate(row_moves) if dk == 0])
    row_mid[:, 1 - k] = log_sum([row_y[i] for i, (dk, _) in enumerate(row_moves) if dk == 1])

    across = [send(row_mid.at[turn(x, d, XS)], row_x.at[i], xs[i]) for i, d in enumerate((2, 1, 3))]
    for copy in cols:
        copy.wait_recv()
    total = log_sum([col[z, k]] + [col_z[i] for i in range(len(col_moves))])
    wide[y] = jnp.where(total > 0.5 * LOW, -0.25 * total + tgt_base[...], kept_pot[...])
    shares = [send(wide.at[y], wide.at[y], ys[i]) for i in range(YS - 1)]
    for copy in across:
        copy.wait_recv()
    ends = log_sum([row_mid[x]] + [row_x[i] for i in range(XS - 1)])
    src_out[:, 0:128] = src_base[:, 0:128] - 0.25 * ends[0]
    src_out[:, 128:256] = src_base[:, 128:256] - 0.25 * ends[1]
    for i, d in enumerate((2, 1, 3)):
        m = used[0] - (YS - 1) + i
        came = wide.at[turn(y, YS - d, YS)]
        pltpu.make_async_remote_copy(
            src_ref=came, dst_ref=came, send_sem=send_sem.at[m], recv_sem=recv_sem.at[m],
            device_id=ys[i], device_id_type=MESH).wait_recv()
    for at in range(YS):
        tgt_out[:, at * 256:(at + 1) * 256] = wide[at]
    for copy in cols + rows + across + shares:
        copy.wait_send()


def settle(row_acc, col_acc, wild, has_row, has_col, src_base, tgt_base, kept_pot):
    vmem = pl.BlockSpec(memory_space=pltpu.VMEM)
    shape = jax.ShapeDtypeStruct
    return pl.pallas_call(
        settle_kernel,
        out_shape=(shape((PER, 256), F32), shape((PER, 1024), F32)),
        in_specs=[vmem] * 8,
        out_specs=(vmem, vmem),
        scratch_shapes=[
            pltpu.VMEM((XS, 2, PER, YS * 128), F32),
            pltpu.VMEM((ZS, 2, PER, 256), F32),
            pltpu.VMEM((7, XS, PER, 128), F32),
            pltpu.VMEM((XS - 1, 2, PER, 128), F32),
            pltpu.VMEM((15, PER, 256), F32),
            pltpu.VMEM((YS, PER, 256), F32),
            pltpu.VMEM((XS, 2, PER, 128), F32),
            pltpu.SemaphoreType.DMA((32,)),
            pltpu.SemaphoreType.DMA((32,)),
        ],
        compiler_params=pltpu.CompilerParams(
            collective_id=1, has_side_effects=True, vmem_limit_bytes=32 * 2**20),
        name="settle",
    )(row_acc, col_acc, wild, has_row, has_col, src_base, tgt_base, kept_pot)


def local(sp, tp, f, g, kept, counts, home):
    src, turned, edges, has_row, has_col, no_row, no_col, src_base, tgt_base, kept_pot = collect(
        jnp.swapaxes(sp, 0, 1), jnp.swapaxes(tp, 0, 1), f, g, kept.T, counts.reshape(1, -1), home.reshape(1, -1))
    row_acc, col_acc, wild = tiles(edges, src, turned, no_row, no_col)
    return settle(row_acc, col_acc, wild, has_row, has_col, src_base, tgt_base, kept_pot)


def solution(mesh):
    placed = (
        P("clusters", None, "tiles"),
        P("clusters", None, None),
        P("clusters", "tiles"),
        P("clusters", None),
        P(),
        P(),
        P(),
    )
    return jax.shard_map(
        local,
        mesh=mesh,
        in_specs=placed,
        out_specs=(P("clusters", "tiles"), P("clusters", None)),
        check_vma=False,
    )
```

```python
import functools

import jax
import jax.numpy as jnp
from jax import lax
from jax.experimental import pallas as pl
from jax.experimental.pallas import tpu as pltpu
from jax.sharding import PartitionSpec as P

MESH = pl.DeviceIdType.MESH
ZS, XS, YS = 8, 4, 4
PER = 8
SHARP = 4.0
EXP2_SCALE = 5.770780163555854
LOW = -1e30
SOURCES, TARGETS = XS * 2 * PER, ZS * 2 * PER
LIST = 256
CHUNK = 2
EARLY = 0
WIDE, SLIM = 32, 8
F32, BF16, I32 = jnp.float32, jnp.bfloat16, jnp.int32


def place():
    c, y = lax.axis_index("clusters"), lax.axis_index("tiles")
    return c // 8, (c // 2) % 4, c % 2, y


def device(z, x, k, y):
    return (z * 8 + x * 2 + k, y)


def iota(shape, dim):
    return lax.broadcasted_iota(I32, shape, dim)


def widen(points, potential, out):
    values = points.astype(F32)
    half_norm = 0.5 * jnp.sum(values * values, axis=0)
    term = potential - half_norm
    high = term.astype(BF16).astype(F32)
    low = (term - high).astype(BF16).astype(F32)
    full = jnp.concatenate([values, high[None], low[None]], axis=0)
    out(jnp.swapaxes(full, 0, 1).astype(BF16))
    return high + low + half_norm


def edge_list(z, x, kept, counts, home, edges_ref, has_row_ref, has_col_ref, no_row_ref, no_col_ref):
    lane = iota((SOURCES, 512), 1)
    row = iota((SOURCES, 512), 0)
    mine = lane == row + z * SOURCES
    count = jnp.sum(jnp.where(mine, counts[...].astype(F32), 0.0), axis=1, keepdims=True)
    names = kept[...].astype(F32)
    lane = lane.astype(F32)
    homes = home[...].astype(F32)
    own_row = iota((SOURCES, 1), 0)
    codes, marks, before, total = [], [], [], jnp.zeros((SOURCES, 1), F32)
    for k in range(12):
        name = jnp.sum(jnp.where(mine, names[k:k + 1], 0.0), axis=1, keepdims=True)
        at = jnp.sum(jnp.where(name == lane, homes, 0.0), axis=1, keepdims=True).astype(I32)
        mark = jnp.where((count > float(k)) & (((at >> 4) & 3) == x), 1.0, 0.0)
        codes.append((own_row * TARGETS + ((at >> 6) << 4) + (at & 15) + 1).astype(F32))
        marks.append(mark)
        before.append(total)
        total = total + mark
    square_row, square_lane = iota((SOURCES, SOURCES), 0), iota((SOURCES, SOURCES), 1)
    across = jnp.sum(jnp.where(square_row == square_lane, total, 0.0), axis=0, keepdims=True)
    ahead = jnp.sum(jnp.where(square_lane < square_row, across, 0.0), axis=1, keepdims=True)
    slot = iota((SOURCES, LIST), 1).astype(F32)
    filled = jnp.zeros((SOURCES, LIST), F32)
    for code, mark, prior in zip(codes, marks, before):
        filled = filled + jnp.where((slot == ahead + prior) & (mark > 0.0), code, 0.0)
    listed = jnp.sum(filled, axis=0, keepdims=True)
    number = jnp.sum(total, axis=0, keepdims=True)
    chosen = jnp.where(listed > 0.0, listed - 1.0, float(SOURCES * TARGETS)).astype(I32)
    edges_ref[...] = jnp.where(iota((8, LIST), 0) == 0, chosen, number.astype(I32))
    has_row = jnp.where(total > 0.0, 1.0, 0.0)
    named = (iota((TARGETS, LIST), 0) == (chosen & (TARGETS - 1))) & (listed > 0.0)
    has_col = jnp.max(jnp.where(named, 1.0, 0.0), axis=1, keepdims=True)
    for has, has_ref, no_ref in ((has_row, has_row_ref, no_row_ref), (has_col, has_col_ref, no_col_ref)):
        has_ref[...] = jnp.broadcast_to(has, has_ref.shape)
        no_ref[...] = jnp.broadcast_to((1.0 - has_ref[...])[:, None, :], no_ref.shape)


def idle_kernel(out):
    out[...] = jnp.zeros(out.shape, F32)


def idle_block():
    return pl.pallas_call(
        idle_kernel,
        out_shape=jax.ShapeDtypeStruct((8, 128), F32),
        out_specs=pl.BlockSpec(memory_space=pltpu.VMEM),
        name="idle",
        cost_estimate=pl.CostEstimate(flops=10**10, bytes_accessed=3 * 10**7, transcendentals=0),
    )()


def collect_kernel(idle, sp, tp, f, g, kept, counts, home,
                   src, turned, edges_ref, has_row_ref, has_col_ref, no_row_ref, no_col_ref, src_base, tgt_base, kept_pot,
                   spare, tgt, send_sem, recv_sem):
    z, x, k, y = place()
    step = lambda at, by, n: lax.rem(at + (by + n), n)

    mate = device(z, x, 1 - k, y)
    xn = {d: device(z, step(x, d, XS), k, y) for d in (1, -1, 2)}
    yn = {d: device(z, x, k, step(y, d, YS)) for d in (1, -1, 2)}
    zn = {d: device(step(z, d, ZS), x, k, y) for d in (1, -1)}

    barrier = pltpu.get_barrier_semaphore()
    for other in (mate, *xn.values(), *yn.values(), *zn.values()):
        pl.semaphore_signal(barrier, inc=1, device_id=other, device_id_type=MESH)

    numbers = {}
    pending = []

    def descriptor(key, ref, to):
        m = numbers.setdefault(key, len(numbers))
        return pltpu.make_async_remote_copy(
            src_ref=ref, dst_ref=ref, send_sem=send_sem.at[m], recv_sem=recv_sem.at[m],
            device_id=to, device_id_type=MESH)

    def send(key, ref, to):
        copy = descriptor(key, ref, to)
        copy.start()
        pending.append(copy)

    def arrive(key, ref):
        descriptor(key, ref, mate).wait_recv()

    def src_block(dx, dy, q, lo=0, n=PER):
        return src.at[step(y, dy, YS), pl.ds(step(x, dx, XS) * 16 + q * 8 + lo, n)]


    def put_target(block):
        tgt[z, k] = block

    quarter = pl.ds(pl.multiple_of(y * 256, 256), 256)
    tgt_base[...] = widen(tp[:, :, quarter], g[:, quarter], put_target)
    kept_pot[...] = g[:, quarter]
    pl.semaphore_wait(barrier, 9)

    def tgt_chunk(dz, c, core):
        return tgt.at[step(z, dz, ZS), core, pl.ds(c * CHUNK, CHUNK)]

    wide_id = iota((32, 256), 0)
    tail_id = iota((16, 256), 0)

    def turn(dz, c, core):
        zz = step(z, dz, ZS)

        def one(i, _):
            block = tgt[zz, core, c * CHUNK + i].astype(F32)
            top = jnp.where(wide_id < 30, block, 1.0)
            low = jnp.where(tail_id >= 14, block[16:32], 0.0)
            turned[zz * 16 + core * 8 + c * CHUNK + i] = jnp.concatenate([top, low], axis=0).T.astype(BF16)
            return 0

        lax.fori_loop(0, CHUNK, one, 0, unroll=CHUNK)

    def take_target(d, dz, c, forward):
        arrive(("z", d, dz + d, c), tgt_chunk(dz, c, k))
        for e in forward:
            send(("z", e, dz, c), tgt_chunk(dz, c, k), zn[e])
        send(("m", dz, c), tgt_chunk(dz, c, k), mate)

    def take_mate(dz, c):
        arrive(("m", dz, c), tgt_chunk(dz, c, 1 - k))
        turn(dz, c, 1 - k)

    def off(q, first, second):
        return (first, second) if q == 0 else (second, first)

    near = {0: (xn, yn), 1: (yn, xn)}

    def first_out(q):
        for d in (1, -1, 2):
            send(("a", q, d), src_block(0, 0, q), near[q][0][d])

    def first_in(q, d):
        arrive(("a", q, d), src_block(*off(q, -d, 0), q))

    def second_out(q, e):
        for d in (1, -1) if e != 2 else (2, 1, -1):
            send(("b", q, e, d), src_block(*off(q, e, 0), q), near[q][1][d])

    def second_in(q, e):
        for d in (1, -1):
            dx, dy = off(q, e, -d)
            arrive(("b", q, e, d), src_block(dx, dy, q))
            if e != 2:
                send(("bf", q, e, d), src_block(dx, dy, q, 0 if d == 1 else 4, 4), near[q][1][d])

    def second_far(q, e):
        dx, dy = off(q, e, 2)
        if e == 2:
            arrive(("b", q, e, 2), src_block(dx, dy, q))
            return
        for d in (1, -1):
            arrive(("bf", q, e, d), src_block(dx, dy, q, 0 if d == 1 else 4, 4))

    def put_source(block):
        halves = block[:, :, 0:128], block[:, :, 128:256]
        src[y, pl.ds(x * 16 + k * 8, PER)] = jnp.where(k == 0, halves[0], halves[1])
        spare[...] = jnp.where(k == 0, halves[1], halves[0])

    chunks = PER // CHUNK
    up = tuple(range(chunks))
    down = up[::-1]

    for c, e in zip(up, down):
        send(("z", 1, 0, c), tgt_chunk(0, c, k), zn[1])
        send(("z", -1, 0, e), tgt_chunk(0, e, k), zn[-1])
    src_base[...] = widen(sp[...], f[...], put_source)
    cross = pltpu.make_async_remote_copy(
        src_ref=spare, dst_ref=src.at[y, pl.ds(x * 16 + k * 8, PER)],
        send_sem=send_sem.at[numbers.setdefault("cross", len(numbers))],
        recv_sem=recv_sem.at[numbers["cross"]], device_id=mate, device_id_type=MESH)
    cross.start()
    pending.append(cross)

    pltpu.make_async_remote_copy(
        src_ref=spare, dst_ref=src.at[y, pl.ds(x * 16 + (1 - k) * 8, PER)],
        send_sem=send_sem.at[numbers["cross"]], recv_sem=recv_sem.at[numbers["cross"]],
        device_id=mate, device_id_type=MESH).wait_recv()
    for q in (0, 1):
        first_out(q)
    for q in (0, 1):
        second_out(q, 0)
    for c in up:
        send(("m", 0, c), tgt_chunk(0, c, k), mate)

    waiting = [(turn, 0, c, k) for c in up] + [(take_mate, 0, c) for c in up]

    def work(n):
        for job in waiting[:n]:
            job[0](*job[1:])
        del waiting[:n]

    def targets_in(hop, c, e):
        for d, dz, at in ((1, -hop, c), (-1, hop, e)):
            if hop < 4 or at in (up[:chunks // 2] if d == 1 else up[chunks // 2:]):
                on = hop < 3 or (hop == 3 and at in (up[:chunks // 2] if d == 1 else up[chunks // 2:]))
                take_target(d, dz, at, (d,) if on else ())
                waiting.append((turn, dz, at, k))
                waiting.append((take_mate, dz, at))

    def sources_in(hop):
        for q in (0, 1):
            if hop == 1:
                for d in (1, -1):
                    first_in(q, d)
                    second_out(q, -d)
            elif hop == 2:
                second_in(q, 0)
                first_in(q, 2)
                second_out(q, 2)
            elif hop == 3:
                second_in(q, 1)
                second_in(q, -1)
            else:
                second_in(q, 2)

    for hop in range(1, 5):
        for i, (c, e) in enumerate(zip(up, down)):
            targets_in(hop, c, e)
            if i == EARLY:
                sources_in(hop)
            if hop == 1 and i == chunks - 1:
                edge_list(z, x, kept, counts, home, edges_ref, has_row_ref, has_col_ref, no_row_ref, no_col_ref)
                for at in range(YS):
                    src[at, SOURCES] = jnp.where(iota((32, 128), 0) == 30, LOW, 0.0).astype(BF16)
            work(4)
    work(len(waiting))
    for q in (0, 1):
        for e in (0, -1, 1, 2):
            second_far(q, e)
    for copy in pending:
        copy.wait_send()


MESSAGES = 128


def collect(sp, tp, f, g, kept, counts, home):
    vmem = pl.BlockSpec(memory_space=pltpu.VMEM)
    shape = jax.ShapeDtypeStruct
    return pl.pallas_call(
        collect_kernel,
        out_shape=(
            shape((YS, SOURCES + 1, 32, 128), BF16),
            shape((TARGETS, 256, 48), BF16),
            shape((8, LIST), I32),
            shape((SOURCES, 128), F32),
            shape((TARGETS, 128), F32),
            shape((SOURCES, 8, 128), F32),
            shape((TARGETS, 8, 128), F32),
            shape((PER, 256), F32),
            shape((PER, 256), F32),
            shape((PER, 256), F32),
        ),
        in_specs=[pl.BlockSpec(memory_space=pl.ANY)] + [vmem] * 7,
        out_specs=(vmem,) * 10,
        scratch_shapes=[
            pltpu.VMEM((PER, 32, 128), BF16),
            pltpu.VMEM((ZS, 2, PER, 32, 256), BF16),
            pltpu.SemaphoreType.DMA((MESSAGES,)),
            pltpu.SemaphoreType.DMA((MESSAGES,)),
        ],
        compiler_params=pltpu.CompilerParams(
            collective_id=0, has_side_effects=True, vmem_limit_bytes=32 * 2**20),
        name="collect",
    )(idle_block(), sp, tp, f, g, kept, counts, home)


def tiles_kernel(edge_vmem, src, turned, no_row, no_col, row_acc, col_acc, wild_ref, edge_ref, edge_sem):
    load = pltpu.make_async_copy(edge_vmem, edge_ref, edge_sem)
    load.start()
    width = turned.shape[1]
    tail = jnp.where(iota((16, YS * 128), 0) >= 14, 1.0, 0.0).astype(BF16)
    row_acc[0:SOURCES] = jnp.concatenate([no_row[...]] * YS, axis=2)
    row_acc[SOURCES] = jnp.zeros((8, YS * 128), F32)
    col_acc[...] = jnp.concatenate([no_col[...]] * 2, axis=2)
    load.wait()
    count = edge_ref[1, 0]

    def scores(s, p):
        cells = jnp.concatenate([src[at, s] for at in range(YS)], axis=1)
        right = jnp.concatenate([cells, tail], axis=0)
        return jnp.dot(turned[p], right, preferred_element_type=F32)

    def edge(at):
        code = edge_ref[0, at]
        s, p = code // TARGETS, code % TARGETS
        e = jnp.exp2(scores(s, p) * EXP2_SCALE)
        q = (e[:, 0:128] + e[:, 128:256]) + (e[:, 256:384] + e[:, 384:512])
        row_acc[s] += e.reshape(width // 8, 8, YS * 128).sum(axis=0)
        col_acc[p] += q.T.reshape(16, 8, width).sum(axis=0)

    def step(start, size):
        def run(it, _):
            for u in range(size):
                edge(start + it * size + u)
            return 0

        return run

    wide = (count + SLIM - 1) // WIDE
    lax.fori_loop(0, wide, step(0, WIDE), 0)
    rest = jnp.maximum(count - wide * WIDE, 0)
    lax.fori_loop(0, (rest + SLIM - 1) // SLIM, step(wide * WIDE, SLIM), 0)

    low = jnp.minimum(jnp.min(row_acc[0:SOURCES]), jnp.min(col_acc[...]))
    high = jnp.maximum(jnp.max(row_acc[0:SOURCES]), jnp.max(col_acc[...]))
    wild = jnp.logical_not((low >= 2.0**-90) & (high <= 2.0**116))
    wild_ref[...] = jnp.where(wild, jnp.ones(wild_ref.shape, F32), 0.0)

    @pl.when(wild)
    def _():
        row_acc[...] = jnp.full(row_acc.shape, LOW, F32)
        col_acc[...] = jnp.full(col_acc.shape, LOW, F32)

        def merge(values, ref, at):
            top = jnp.max(values, axis=0, keepdims=True)
            here = top + jnp.log(jnp.sum(jnp.exp(values - top), axis=0, keepdims=True))
            old = ref[at, 0:1, :]
            peak = jnp.maximum(here, old)
            ref[at, 0:1, :] = peak + jnp.log(jnp.exp(here - peak) + jnp.exp(old - peak))

        def careful(e, _):
            code = edge_ref[0, e]
            s, p = code // TARGETS, code % TARGETS
            value = SHARP * scores(s, p)
            merge(value, row_acc, s)
            merge(value.T, col_acc, p)
            return 0

        lax.fori_loop(0, count, careful, 0)


def tiles(edges, src, turned, no_row, no_col):
    vmem = pl.BlockSpec(memory_space=pltpu.VMEM)
    shape = jax.ShapeDtypeStruct
    return pl.pallas_call(
        tiles_kernel,
        out_shape=(
            shape((SOURCES + 1, 8, YS * 128), F32),
            shape((TARGETS, 8, 256), F32),
            shape((8, 128), F32),
        ),
        in_specs=[vmem] * 5,
        out_specs=(vmem,) * 3,
        scratch_shapes=[
            pltpu.SMEM((8, LIST), I32),
            pltpu.SemaphoreType.DMA,
        ],
        compiler_params=pltpu.CompilerParams(vmem_limit_bytes=32 * 2**20),
        name="tiles",
    )(edges, src, turned, no_row, no_col)


def log_sum(parts):
    top = functools.reduce(jnp.maximum, parts)
    return top + jnp.log(sum(jnp.exp(part - top) for part in parts))


def settle_kernel(row_acc, col_acc, wild_ref, has_row, has_col, src_base, tgt_base, kept_pot, src_out, tgt_out,
                  row, col, row_y, row_x, col_z, wide, row_mid, send_sem, recv_sem):
    z, x, k, y = place()
    turn = lambda at, by, n: lax.rem(at + by, n)
    row_moves = [(dk, dy) for dk in (1, 0) for dy in (2, 1, 3, 0) if dk or dy]
    col_moves = [(dz, dk) for dz in (4, 3, 5, 2, 6, 1, 7, 0) for dk in (1, 0) if dz or dk]
    core = lambda dk: turn(k, dk, 2)
    xs = [device(z, turn(x, d, XS), k, y) for d in (2, 1, 3)]
    ys = [device(z, x, k, turn(y, d, YS)) for d in (2, 1, 3)]
    row_to = [device(z, x, core(dk), turn(y, dy, YS)) for dk, dy in row_moves]
    col_to = [device(turn(z, dz, ZS), x, core(dk), y) for dz, dk in col_moves]
    barrier = pltpu.get_barrier_semaphore()
    everyone = [to for to, (dz, dk) in zip(col_to, col_moves) if dz] + row_to + xs
    for other in everyone:
        pl.semaphore_signal(barrier, inc=1, device_id=other, device_id_type=MESH)

    wild = wild_ref[0:1, 0:1] > 0.0

    def logs(acc, has, out):
        has = has[:, 0:1] > 0.0
        total = jnp.where(has, jnp.sum(acc, axis=1), 1.0)
        out[...] = jnp.where(has, jnp.where(wild, acc[:, 0], jnp.log(total)), LOW).reshape(out.shape)

    logs(row_acc[0:SOURCES], has_row, row)
    logs(col_acc[...], has_col, col)
    pl.semaphore_wait(barrier, len(everyone))
    used = [0]

    def send(src_ref, dst_ref, to):
        m = used[0]
        used[0] += 1
        copy = pltpu.make_async_remote_copy(
            src_ref=src_ref, dst_ref=dst_ref, send_sem=send_sem.at[m], recv_sem=recv_sem.at[m],
            device_id=to, device_id_type=MESH)
        copy.start()
        return copy

    def quarter(at):
        return pl.ds(pl.multiple_of(at * 128, 128), 128)

    cols = [send(col.at[turn(z, dz, ZS), core(dk)], col_z.at[i], col_to[i]) for i, (dz, dk) in enumerate(col_moves)]
    rows = [send(row.at[:, core(dk), :, quarter(turn(y, dy, YS))], row_y.at[i], row_to[i])
            for i, (dk, dy) in enumerate(row_moves)]
    for copy in rows:
        copy.wait_recv()
    own = row[:, k, :, quarter(y)]
    row_mid[:, k] = log_sum([own] + [row_y[i] for i, (dk, _) in enumerate(row_moves) if dk == 0])
    row_mid[:, 1 - k] = log_sum([row_y[i] for i, (dk, _) in enumerate(row_moves) if dk == 1])

    across = [send(row_mid.at[turn(x, d, XS)], row_x.at[i], xs[i]) for i, d in enumerate((2, 1, 3))]
    for copy in cols:
        copy.wait_recv()
    total = log_sum([col[z, k]] + [col_z[i] for i in range(len(col_moves))])
    wide[y] = jnp.where(total > 0.5 * LOW, -0.25 * total + tgt_base[...], kept_pot[...])
    shares = [send(wide.at[y], wide.at[y], ys[i]) for i in range(YS - 1)]
    for copy in across:
        copy.wait_recv()
    ends = log_sum([row_mid[x]] + [row_x[i] for i in range(XS - 1)])
    src_out[:, 0:128] = src_base[:, 0:128] - 0.25 * ends[0]
    src_out[:, 128:256] = src_base[:, 128:256] - 0.25 * ends[1]
    for i, d in enumerate((2, 1, 3)):
        m = used[0] - (YS - 1) + i
        came = wide.at[turn(y, YS - d, YS)]
        pltpu.make_async_remote_copy(
            src_ref=came, dst_ref=came, send_sem=send_sem.at[m], recv_sem=recv_sem.at[m],
            device_id=ys[i], device_id_type=MESH).wait_recv()
    for at in range(YS):
        tgt_out[:, at * 256:(at + 1) * 256] = wide[at]
    for copy in cols + rows + across + shares:
        copy.wait_send()


def settle(row_acc, col_acc, wild, has_row, has_col, src_base, tgt_base, kept_pot):
    vmem = pl.BlockSpec(memory_space=pltpu.VMEM)
    shape = jax.ShapeDtypeStruct
    return pl.pallas_call(
        settle_kernel,
        out_shape=(shape((PER, 256), F32), shape((PER, 1024), F32)),
        in_specs=[vmem] * 8,
        out_specs=(vmem, vmem),
        scratch_shapes=[
            pltpu.VMEM((XS, 2, PER, YS * 128), F32),
            pltpu.VMEM((ZS, 2, PER, 256), F32),
            pltpu.VMEM((7, XS, PER, 128), F32),
            pltpu.VMEM((XS - 1, 2, PER, 128), F32),
            pltpu.VMEM((15, PER, 256), F32),
            pltpu.VMEM((YS, PER, 256), F32),
            pltpu.VMEM((XS, 2, PER, 128), F32),
            pltpu.SemaphoreType.DMA((32,)),
            pltpu.SemaphoreType.DMA((32,)),
        ],
        compiler_params=pltpu.CompilerParams(
            collective_id=1, has_side_effects=True, vmem_limit_bytes=32 * 2**20),
        name="settle",
    )(row_acc, col_acc, wild, has_row, has_col, src_base, tgt_base, kept_pot)


def local(sp, tp, f, g, kept, counts, home):
    src, turned, edges, has_row, has_col, no_row, no_col, src_base, tgt_base, kept_pot = collect(
        jnp.swapaxes(sp, 0, 1), jnp.swapaxes(tp, 0, 1), f, g, kept.T, counts.reshape(1, -1), home.reshape(1, -1))
    row_acc, col_acc, wild = tiles(edges, src, turned, no_row, no_col)
    return settle(row_acc, col_acc, wild, has_row, has_col, src_base, tgt_base, kept_pot)


def solution(mesh):
    placed = (
        P("clusters", None, "tiles"),
        P("clusters", None, None),
        P("clusters", "tiles"),
        P("clusters", None),
        P(),
        P(),
        P(),
    )
    return jax.shard_map(
        local,
        mesh=mesh,
        in_specs=placed,
        out_specs=(P("clusters", "tiles"), P("clusters", None)),
        check_vma=False,
    )
```

```python
import functools

import jax
import jax.numpy as jnp
from jax import lax
from jax.experimental import pallas as pl
from jax.experimental.pallas import tpu as pltpu
from jax.sharding import PartitionSpec as P

MESH = pl.DeviceIdType.MESH
ZS, XS, YS = 8, 4, 4
PER = 8
SHARP = 4.0
EXP2_SCALE = 5.770780163555854
LOW = -1e30
SOURCES, TARGETS = XS * 2 * PER, ZS * 2 * PER
LIST = 256
CHUNK = 2
EARLY = 0
WIDE, SLIM = 32, 8
F32, BF16, I32 = jnp.float32, jnp.bfloat16, jnp.int32


def place():
    c, y = lax.axis_index("clusters"), lax.axis_index("tiles")
    return c // 8, (c // 2) % 4, c % 2, y


def device(z, x, k, y):
    return (z * 8 + x * 2 + k, y)


def iota(shape, dim):
    return lax.broadcasted_iota(I32, shape, dim)


def widen(points, potential, out):
    values = points.astype(F32)
    half_norm = 0.5 * jnp.sum(values * values, axis=0)
    term = potential - half_norm
    high = term.astype(BF16).astype(F32)
    low = (term - high).astype(BF16).astype(F32)
    full = jnp.concatenate([values, high[None], low[None]], axis=0)
    out(jnp.swapaxes(full, 0, 1).astype(BF16))
    return high + low + half_norm


def edge_list(z, x, kept, counts, home, edges_ref, has_row_ref, has_col_ref, no_row_ref, no_col_ref):
    lane = iota((SOURCES, 512), 1)
    row = iota((SOURCES, 512), 0)
    mine = lane == row + z * SOURCES
    count = jnp.sum(jnp.where(mine, counts[...].astype(F32), 0.0), axis=1, keepdims=True)
    names = kept[...].astype(F32)
    lane = lane.astype(F32)
    homes = home[...].astype(F32)
    own_row = iota((SOURCES, 1), 0)
    codes, marks, before, total = [], [], [], jnp.zeros((SOURCES, 1), F32)
    for k in range(12):
        name = jnp.sum(jnp.where(mine, names[k:k + 1], 0.0), axis=1, keepdims=True)
        at = jnp.sum(jnp.where(name == lane, homes, 0.0), axis=1, keepdims=True).astype(I32)
        mark = jnp.where((count > float(k)) & (((at >> 4) & 3) == x), 1.0, 0.0)
        codes.append((own_row * TARGETS + ((at >> 6) << 4) + (at & 15) + 1).astype(F32))
        marks.append(mark)
        before.append(total)
        total = total + mark
    square_row, square_lane = iota((SOURCES, SOURCES), 0), iota((SOURCES, SOURCES), 1)
    across = jnp.sum(jnp.where(square_row == square_lane, total, 0.0), axis=0, keepdims=True)
    ahead = jnp.sum(jnp.where(square_lane < square_row, across, 0.0), axis=1, keepdims=True)
    slot = iota((SOURCES, LIST), 1).astype(F32)
    filled = jnp.zeros((SOURCES, LIST), F32)
    for code, mark, prior in zip(codes, marks, before):
        filled = filled + jnp.where((slot == ahead + prior) & (mark > 0.0), code, 0.0)
    listed = jnp.sum(filled, axis=0, keepdims=True)
    number = jnp.sum(total, axis=0, keepdims=True)
    chosen = jnp.where(listed > 0.0, listed - 1.0, float(SOURCES * TARGETS)).astype(I32)
    edges_ref[...] = jnp.where(iota((8, LIST), 0) == 0, chosen, number.astype(I32))
    has_row = jnp.where(total > 0.0, 1.0, 0.0)
    named = (iota((TARGETS, LIST), 0) == (chosen & (TARGETS - 1))) & (listed > 0.0)
    has_col = jnp.max(jnp.where(named, 1.0, 0.0), axis=1, keepdims=True)
    for has, has_ref, no_ref in ((has_row, has_row_ref, no_row_ref), (has_col, has_col_ref, no_col_ref)):
        has_ref[...] = jnp.broadcast_to(has, has_ref.shape)
        no_ref[...] = jnp.broadcast_to((1.0 - has_ref[...])[:, None, :], no_ref.shape)


def idle_kernel(out):
    out[...] = jnp.zeros(out.shape, F32)


def idle_block():
    return pl.pallas_call(
        idle_kernel,
        out_shape=jax.ShapeDtypeStruct((8, 128), F32),
        out_specs=pl.BlockSpec(memory_space=pltpu.VMEM),
        name="idle",
        cost_estimate=pl.CostEstimate(flops=10**10, bytes_accessed=3 * 10**7, transcendentals=0),
    )()


def collect_kernel(idle, sp, tp, f, g, kept, counts, home,
                   src, turned, edges_ref, has_row_ref, has_col_ref, no_row_ref, no_col_ref, src_base, tgt_base, kept_pot,
                   spare, tgt, send_sem, recv_sem):
    z, x, k, y = place()
    step = lambda at, by, n: lax.rem(at + (by + n), n)

    mate = device(z, x, 1 - k, y)
    xn = {d: device(z, step(x, d, XS), k, y) for d in (1, -1, 2)}
    yn = {d: device(z, x, k, step(y, d, YS)) for d in (1, -1, 2)}
    zn = {d: device(step(z, d, ZS), x, k, y) for d in (1, -1)}

    barrier = pltpu.get_barrier_semaphore()
    for other in (mate, *xn.values(), *yn.values(), *zn.values()):
        pl.semaphore_signal(barrier, inc=1, device_id=other, device_id_type=MESH)

    numbers = {}
    pending = []

    def descriptor(key, ref, to):
        m = numbers.setdefault(key, len(numbers))
        return pltpu.make_async_remote_copy(
            src_ref=ref, dst_ref=ref, send_sem=send_sem.at[m], recv_sem=recv_sem.at[m],
            device_id=to, device_id_type=MESH)

    def send(key, ref, to):
        copy = descriptor(key, ref, to)
        copy.start()
        pending.append(copy)

    def arrive(key, ref):
        descriptor(key, ref, mate).wait_recv()

    def src_block(dx, dy, q, lo=0, n=PER):
        return src.at[step(y, dy, YS), pl.ds(step(x, dx, XS) * 16 + q * 8 + lo, n)]


    def put_target(block):
        tgt[z, k] = block

    quarter = pl.ds(pl.multiple_of(y * 256, 256), 256)
    tgt_base[...] = widen(tp[:, :, quarter], g[:, quarter], put_target)
    kept_pot[...] = g[:, quarter]
    pl.semaphore_wait(barrier, 9)

    def tgt_chunk(dz, c, core):
        return tgt.at[step(z, dz, ZS), core, pl.ds(c * CHUNK, CHUNK)]

    wide_id = iota((32, 256), 0)
    tail_id = iota((16, 256), 0)

    def turn(dz, c, core):
        zz = step(z, dz, ZS)

        def one(i, _):
            block = tgt[zz, core, c * CHUNK + i].astype(F32)
            top = jnp.where(wide_id < 30, block, 1.0)
            low = jnp.where(tail_id >= 14, block[16:32], 0.0)
            turned[zz * 16 + core * 8 + c * CHUNK + i] = jnp.concatenate([top, low], axis=0).T.astype(BF16)
            return 0

        lax.fori_loop(0, CHUNK, one, 0, unroll=CHUNK)

    def take_target(d, dz, c, forward):
        arrive(("z", d, dz + d, c), tgt_chunk(dz, c, k))
        for e in forward:
            send(("z", e, dz, c), tgt_chunk(dz, c, k), zn[e])
        send(("m", dz, c), tgt_chunk(dz, c, k), mate)

    def take_mate(dz, c):
        arrive(("m", dz, c), tgt_chunk(dz, c, 1 - k))
        turn(dz, c, 1 - k)

    def off(q, first, second):
        return (first, second) if q == 0 else (second, first)

    near = {0: (xn, yn), 1: (yn, xn)}

    def first_out(q):
        for d in (1, -1, 2):
            send(("a", q, d), src_block(0, 0, q), near[q][0][d])

    def first_in(q, d):
        arrive(("a", q, d), src_block(*off(q, -d, 0), q))

    def second_out(q, e):
        for d in (1, -1) if e != 2 else (2, 1, -1):
            send(("b", q, e, d), src_block(*off(q, e, 0), q), near[q][1][d])

    def second_in(q, e):
        for d in (1, -1):
            dx, dy = off(q, e, -d)
            arrive(("b", q, e, d), src_block(dx, dy, q))
            if e != 2:
                send(("bf", q, e, d), src_block(dx, dy, q, 0 if d == 1 else 4, 4), near[q][1][d])

    def second_far(q, e):
        dx, dy = off(q, e, 2)
        if e == 2:
            arrive(("b", q, e, 2), src_block(dx, dy, q))
            return
        for d in (1, -1):
            arrive(("bf", q, e, d), src_block(dx, dy, q, 0 if d == 1 else 4, 4))

    def put_source(block):
        halves = block[:, :, 0:128], block[:, :, 128:256]
        src[y, pl.ds(x * 16 + k * 8, PER)] = jnp.where(k == 0, halves[0], halves[1])
        spare[...] = jnp.where(k == 0, halves[1], halves[0])

    chunks = PER // CHUNK
    up = tuple(range(chunks))
    down = up[::-1]

    for c, e in zip(up, down):
        send(("z", 1, 0, c), tgt_chunk(0, c, k), zn[1])
        send(("z", -1, 0, e), tgt_chunk(0, e, k), zn[-1])
    src_base[...] = widen(sp[...], f[...], put_source)
    cross = pltpu.make_async_remote_copy(
        src_ref=spare, dst_ref=src.at[y, pl.ds(x * 16 + k * 8, PER)],
        send_sem=send_sem.at[numbers.setdefault("cross", len(numbers))],
        recv_sem=recv_sem.at[numbers["cross"]], device_id=mate, device_id_type=MESH)
    cross.start()
    pending.append(cross)

    pltpu.make_async_remote_copy(
        src_ref=spare, dst_ref=src.at[y, pl.ds(x * 16 + (1 - k) * 8, PER)],
        send_sem=send_sem.at[numbers["cross"]], recv_sem=recv_sem.at[numbers["cross"]],
        device_id=mate, device_id_type=MESH).wait_recv()
    for q in (0, 1):
        first_out(q)
    for q in (0, 1):
        second_out(q, 0)
    for c in up:
        send(("m", 0, c), tgt_chunk(0, c, k), mate)

    waiting = [(turn, 0, c, k) for c in up] + [(take_mate, 0, c) for c in up]

    def work(n):
        for job in waiting[:n]:
            job[0](*job[1:])
        del waiting[:n]

    def targets_in(hop, c, e):
        for d, dz, at in ((1, -hop, c), (-1, hop, e)):
            if hop < 4 or at in (up[:chunks // 2] if d == 1 else up[chunks // 2:]):
                on = hop < 3 or (hop == 3 and at in (up[:chunks // 2] if d == 1 else up[chunks // 2:]))
                take_target(d, dz, at, (d,) if on else ())
                waiting.append((turn, dz, at, k))
                waiting.append((take_mate, dz, at))

    def sources_in(hop):
        for q in (0, 1):
            if hop == 1:
                for d in (1, -1):
                    first_in(q, d)
                    second_out(q, -d)
            elif hop == 2:
                second_in(q, 0)
                first_in(q, 2)
                second_out(q, 2)
            elif hop == 3:
                second_in(q, 1)
                second_in(q, -1)
            else:
                second_in(q, 2)

    for hop in range(1, 5):
        for i, (c, e) in enumerate(zip(up, down)):
            targets_in(hop, c, e)
            if i == EARLY:
                sources_in(hop)
            if hop == 1 and i == chunks - 1:
                edge_list(z, x, kept, counts, home, edges_ref, has_row_ref, has_col_ref, no_row_ref, no_col_ref)
                for at in range(YS):
                    src[at, SOURCES] = jnp.where(iota((32, 128), 0) == 30, LOW, 0.0).astype(BF16)
            work(5 if hop == 3 else 4)
    work(len(waiting))
    for q in (0, 1):
        for e in (0, -1, 1, 2):
            second_far(q, e)
    for copy in pending:
        copy.wait_send()


MESSAGES = 128


def collect(sp, tp, f, g, kept, counts, home):
    vmem = pl.BlockSpec(memory_space=pltpu.VMEM)
    shape = jax.ShapeDtypeStruct
    return pl.pallas_call(
        collect_kernel,
        out_shape=(
            shape((YS, SOURCES + 1, 32, 128), BF16),
            shape((TARGETS, 256, 48), BF16),
            shape((8, LIST), I32),
            shape((SOURCES, 128), F32),
            shape((TARGETS, 128), F32),
            shape((SOURCES, 8, 128), F32),
            shape((TARGETS, 8, 128), F32),
            shape((PER, 256), F32),
            shape((PER, 256), F32),
            shape((PER, 256), F32),
        ),
        in_specs=[pl.BlockSpec(memory_space=pl.ANY)] + [vmem] * 7,
        out_specs=(vmem,) * 10,
        scratch_shapes=[
            pltpu.VMEM((PER, 32, 128), BF16),
            pltpu.VMEM((ZS, 2, PER, 32, 256), BF16),
            pltpu.SemaphoreType.DMA((MESSAGES,)),
            pltpu.SemaphoreType.DMA((MESSAGES,)),
        ],
        compiler_params=pltpu.CompilerParams(
            collective_id=0, has_side_effects=True, vmem_limit_bytes=32 * 2**20),
        name="collect",
    )(idle_block(), sp, tp, f, g, kept, counts, home)


def tiles_kernel(edge_vmem, src, turned, no_row, no_col, row_acc, col_acc, wild_ref, edge_ref, edge_sem):
    load = pltpu.make_async_copy(edge_vmem, edge_ref, edge_sem)
    load.start()
    width = turned.shape[1]
    tail = jnp.where(iota((16, YS * 128), 0) >= 14, 1.0, 0.0).astype(BF16)
    row_acc[0:SOURCES] = jnp.concatenate([no_row[...]] * YS, axis=2)
    row_acc[SOURCES] = jnp.zeros((8, YS * 128), F32)
    col_acc[...] = jnp.concatenate([no_col[...]] * 2, axis=2)
    load.wait()
    count = edge_ref[1, 0]

    def scores(s, p):
        cells = jnp.concatenate([src[at, s] for at in range(YS)], axis=1)
        right = jnp.concatenate([cells, tail], axis=0)
        return jnp.dot(turned[p], right, preferred_element_type=F32)

    def edge(at):
        code = edge_ref[0, at]
        s, p = code // TARGETS, code % TARGETS
        e = jnp.exp2(scores(s, p) * EXP2_SCALE)
        q = (e[:, 0:128] + e[:, 128:256]) + (e[:, 256:384] + e[:, 384:512])
        row_acc[s] += e.reshape(width // 8, 8, YS * 128).sum(axis=0)
        col_acc[p] += q.T.reshape(16, 8, width).sum(axis=0)

    def step(start, size):
        def run(it, _):
            for u in range(size):
                edge(start + it * size + u)
            return 0

        return run

    wide = (count + SLIM - 1) // WIDE
    lax.fori_loop(0, wide, step(0, WIDE), 0)
    rest = jnp.maximum(count - wide * WIDE, 0)
    lax.fori_loop(0, (rest + SLIM - 1) // SLIM, step(wide * WIDE, SLIM), 0)

    low = jnp.minimum(jnp.min(row_acc[0:SOURCES]), jnp.min(col_acc[...]))
    high = jnp.maximum(jnp.max(row_acc[0:SOURCES]), jnp.max(col_acc[...]))
    wild = jnp.logical_not((low >= 2.0**-90) & (high <= 2.0**116))
    wild_ref[...] = jnp.where(wild, jnp.ones(wild_ref.shape, F32), 0.0)

    @pl.when(wild)
    def _():
        row_acc[...] = jnp.full(row_acc.shape, LOW, F32)
        col_acc[...] = jnp.full(col_acc.shape, LOW, F32)

        def merge(values, ref, at):
            top = jnp.max(values, axis=0, keepdims=True)
            here = top + jnp.log(jnp.sum(jnp.exp(values - top), axis=0, keepdims=True))
            old = ref[at, 0:1, :]
            peak = jnp.maximum(here, old)
            ref[at, 0:1, :] = peak + jnp.log(jnp.exp(here - peak) + jnp.exp(old - peak))

        def careful(e, _):
            code = edge_ref[0, e]
            s, p = code // TARGETS, code % TARGETS
            value = SHARP * scores(s, p)
            merge(value, row_acc, s)
            merge(value.T, col_acc, p)
            return 0

        lax.fori_loop(0, count, careful, 0)


def tiles(edges, src, turned, no_row, no_col):
    vmem = pl.BlockSpec(memory_space=pltpu.VMEM)
    shape = jax.ShapeDtypeStruct
    return pl.pallas_call(
        tiles_kernel,
        out_shape=(
            shape((SOURCES + 1, 8, YS * 128), F32),
            shape((TARGETS, 8, 256), F32),
            shape((8, 128), F32),
        ),
        in_specs=[vmem] * 5,
        out_specs=(vmem,) * 3,
        scratch_shapes=[
            pltpu.SMEM((8, LIST), I32),
            pltpu.SemaphoreType.DMA,
        ],
        compiler_params=pltpu.CompilerParams(vmem_limit_bytes=32 * 2**20),
        name="tiles",
    )(edges, src, turned, no_row, no_col)


def log_sum(parts):
    top = functools.reduce(jnp.maximum, parts)
    return top + jnp.log(sum(jnp.exp(part - top) for part in parts))


def settle_kernel(row_acc, col_acc, wild_ref, has_row, has_col, src_base, tgt_base, kept_pot, src_out, tgt_out,
                  row, col, row_y, row_x, col_z, wide, row_mid, send_sem, recv_sem):
    z, x, k, y = place()
    turn = lambda at, by, n: lax.rem(at + by, n)
    row_moves = [(dk, dy) for dk in (1, 0) for dy in (2, 1, 3, 0) if dk or dy]
    col_moves = [(dz, dk) for dz in (4, 3, 5, 2, 6, 1, 7, 0) for dk in (1, 0) if dz or dk]
    core = lambda dk: turn(k, dk, 2)
    xs = [device(z, turn(x, d, XS), k, y) for d in (2, 1, 3)]
    ys = [device(z, x, k, turn(y, d, YS)) for d in (2, 1, 3)]
    row_to = [device(z, x, core(dk), turn(y, dy, YS)) for dk, dy in row_moves]
    col_to = [device(turn(z, dz, ZS), x, core(dk), y) for dz, dk in col_moves]
    barrier = pltpu.get_barrier_semaphore()
    everyone = [to for to, (dz, dk) in zip(col_to, col_moves) if dz] + row_to + xs
    for other in everyone:
        pl.semaphore_signal(barrier, inc=1, device_id=other, device_id_type=MESH)

    wild = wild_ref[0:1, 0:1] > 0.0

    def logs(acc, has, out):
        has = has[:, 0:1] > 0.0
        total = jnp.where(has, jnp.sum(acc, axis=1), 1.0)
        out[...] = jnp.where(has, jnp.where(wild, acc[:, 0], jnp.log(total)), LOW).reshape(out.shape)

    logs(row_acc[0:SOURCES], has_row, row)
    logs(col_acc[...], has_col, col)
    pl.semaphore_wait(barrier, len(everyone))
    used = [0]

    def send(src_ref, dst_ref, to):
        m = used[0]
        used[0] += 1
        copy = pltpu.make_async_remote_copy(
            src_ref=src_ref, dst_ref=dst_ref, send_sem=send_sem.at[m], recv_sem=recv_sem.at[m],
            device_id=to, device_id_type=MESH)
        copy.start()
        return copy

    def quarter(at):
        return pl.ds(pl.multiple_of(at * 128, 128), 128)

    cols = [send(col.at[turn(z, dz, ZS), core(dk)], col_z.at[i], col_to[i]) for i, (dz, dk) in enumerate(col_moves)]
    rows = [send(row.at[:, core(dk), :, quarter(turn(y, dy, YS))], row_y.at[i], row_to[i])
            for i, (dk, dy) in enumerate(row_moves)]
    for copy in rows:
        copy.wait_recv()
    own = row[:, k, :, quarter(y)]
    row_mid[:, k] = log_sum([own] + [row_y[i] for i, (dk, _) in enumerate(row_moves) if dk == 0])
    row_mid[:, 1 - k] = log_sum([row_y[i] for i, (dk, _) in enumerate(row_moves) if dk == 1])

    across = [send(row_mid.at[turn(x, d, XS)], row_x.at[i], xs[i]) for i, d in enumerate((2, 1, 3))]
    for copy in cols:
        copy.wait_recv()
    total = log_sum([col[z, k]] + [col_z[i] for i in range(len(col_moves))])
    wide[y] = jnp.where(total > 0.5 * LOW, -0.25 * total + tgt_base[...], kept_pot[...])
    shares = [send(wide.at[y], wide.at[y], ys[i]) for i in range(YS - 1)]
    for copy in across:
        copy.wait_recv()
    ends = log_sum([row_mid[x]] + [row_x[i] for i in range(XS - 1)])
    src_out[:, 0:128] = src_base[:, 0:128] - 0.25 * ends[0]
    src_out[:, 128:256] = src_base[:, 128:256] - 0.25 * ends[1]
    for i, d in enumerate((2, 1, 3)):
        m = used[0] - (YS - 1) + i
        came = wide.at[turn(y, YS - d, YS)]
        pltpu.make_async_remote_copy(
            src_ref=came, dst_ref=came, send_sem=send_sem.at[m], recv_sem=recv_sem.at[m],
            device_id=ys[i], device_id_type=MESH).wait_recv()
    for at in range(YS):
        tgt_out[:, at * 256:(at + 1) * 256] = wide[at]
    for copy in cols + rows + across + shares:
        copy.wait_send()


def settle(row_acc, col_acc, wild, has_row, has_col, src_base, tgt_base, kept_pot):
    vmem = pl.BlockSpec(memory_space=pltpu.VMEM)
    shape = jax.ShapeDtypeStruct
    return pl.pallas_call(
        settle_kernel,
        out_shape=(shape((PER, 256), F32), shape((PER, 1024), F32)),
        in_specs=[vmem] * 8,
        out_specs=(vmem, vmem),
        scratch_shapes=[
            pltpu.VMEM((XS, 2, PER, YS * 128), F32),
            pltpu.VMEM((ZS, 2, PER, 256), F32),
            pltpu.VMEM((7, XS, PER, 128), F32),
            pltpu.VMEM((XS - 1, 2, PER, 128), F32),
            pltpu.VMEM((15, PER, 256), F32),
            pltpu.VMEM((YS, PER, 256), F32),
            pltpu.VMEM((XS, 2, PER, 128), F32),
            pltpu.SemaphoreType.DMA((32,)),
            pltpu.SemaphoreType.DMA((32,)),
        ],
        compiler_params=pltpu.CompilerParams(
            collective_id=1, has_side_effects=True, vmem_limit_bytes=32 * 2**20),
        name="settle",
    )(row_acc, col_acc, wild, has_row, has_col, src_base, tgt_base, kept_pot)


def local(sp, tp, f, g, kept, counts, home):
    src, turned, edges, has_row, has_col, no_row, no_col, src_base, tgt_base, kept_pot = collect(
        jnp.swapaxes(sp, 0, 1), jnp.swapaxes(tp, 0, 1), f, g, kept.T, counts.reshape(1, -1), home.reshape(1, -1))
    row_acc, col_acc, wild = tiles(edges, src, turned, no_row, no_col)
    return settle(row_acc, col_acc, wild, has_row, has_col, src_base, tgt_base, kept_pot)


def solution(mesh):
    placed = (
        P("clusters", None, "tiles"),
        P("clusters", None, None),
        P("clusters", "tiles"),
        P("clusters", None),
        P(),
        P(),
        P(),
    )
    return jax.shard_map(
        local,
        mesh=mesh,
        in_specs=placed,
        out_specs=(P("clusters", "tiles"), P("clusters", None)),
        check_vma=False,
    )
```
